32 devices in a mesh: fsdp: 8 (over z, y), heads: 4 (over x, core).
Axes of the slice: x: 2, y: 2, z: 4, core: 2. Of those that a mesh axis runs over, the one named last changes fastest.
Arguments:
- activations: bfloat16 [1024, 2048], P('fsdp'), may hold values from -6 to 6
- norm_gains: bfloat16 [2, 2048], P(None, 'fsdp'), may hold values from 0.099609375 to 1.8984375
- w_query: bfloat16 [2048, 4, 512], P('fsdp', 'heads'), may hold values from -0.125 to 0.125
- w_keyval: bfloat16 [2048, 4, 128], P('fsdp', 'heads'), may hold values from -0.125 to 0.125
- w_out: bfloat16 [4, 512, 2048], P('heads', None, 'fsdp'), may hold values from -0.375 to 0.375
- w_gateup: bfloat16 [2048, 2, 5632], P('fsdp', None, 'heads'), may hold values from -0.125 to 0.125
- w_down: bfloat16 [5632, 2048], P('heads', 'fsdp'), may hold values from -0.078125 to 0.078125
- seq_lengths: int32 [3], replicated, may hold values from 1 to 512, 1024 in all
- token_slot: int32 [1024], P('fsdp'), may hold values from 0 to 1023, as said below
- out_grad: bfloat16 [1024, 2048], P('fsdp'), may hold values from -6 to 6
Outputs:
- block_out: bfloat16 [1024, 2048], P('fsdp')
- input_grad: float32 [1024, 2048], P('fsdp')
- grad_gains: float32 [2, 2048], P(None, 'fsdp')
- grad_query: float32 [2048, 4, 512], P('fsdp', 'heads')
- grad_keyval: float32 [2048, 4, 128], P('fsdp', 'heads')
- grad_out: float32 [4, 512, 2048], P('heads', None, 'fsdp')
- grad_gateup: float32 [2048, 2, 5632], P('fsdp', None, 'heads')
- grad_down: float32 [5632, 2048], P('heads', 'fsdp')
The draws below stay inside these ranges and needn't reach their ends.
Inputs may be any that keep to these rules, and one draw needn't show every extreme that they name: `seq_lengths`: the lengths sum to 1024; the longest is exactly 512. `token_slot`: A permutation of the pack's places. Each device of fsdp holds exactly one place of every aligned block of 8 consecutive places, and its places rise with the row.
All inputs are finite; a program needn't handle non-finite values.
Results may differ from the reference program's by a relative error of at most 0.02.
Values may be sent and summed in bfloat16 or wider, within the bound.
No kernel may reach another device: no remote copies, remote signals or barrier semaphores. Data moves between devices by JAX's collectives and lax.ppermute only.
A program may use at most 128 MiB of HBM per device.

```python
import math
import jax
import jax.numpy as jnp
import numpy as np
from jax import lax

D = 2048
HEADS = 32
KV_HEADS = 4
HD = 64
FF = 5632
TOK_DEV = 128
TOKENS = 1024
MAX_LEN = 512
NSEQ = 3


def draw_token_slot(key, part):
    key = jax.random.fold_in(key, 11)
    devices = TOKENS // TOK_DEV
    shifts = jax.random.randint(key, (TOK_DEV,), 0, devices)
    device_ids = jnp.arange(devices, dtype=jnp.int32)[:, None]
    rounds = jnp.arange(TOK_DEV, dtype=jnp.int32)[None, :]
    slots = rounds * devices + (device_ids - shifts[None, :]) % devices
    return slots.reshape(TOKENS).astype(jnp.int32)


def level_of(own_key, shape, split, low, top_value):
    gain = 1.0
    for dim, parts in split:
        heights = jax.random.uniform(jax.random.fold_in(jax.random.fold_in(own_key, 6), dim), (parts,), jnp.float32, low / len(split), top_value / len(split))
        gain = gain * jnp.repeat(jnp.exp(heights), shape[dim] // parts).reshape((-1,) + (1,) * (len(shape) - 1 - dim))
    return gain


def split_up(count, total, reach, lean):
    weights = [(1 << 20) // math.isqrt(rank ** lean) + 1 for rank in range(2, count + 1)]
    spare, holding = total - reach - (count - 1), [1] * (count - 1)
    while spare > 0:
        movable = [i for i in range(count - 1) if holding[i] < reach]
        whole, left = sum([weights[i] for i in movable]), spare
        for i in movable:
            extra = min(reach - holding[i], max(1, left * weights[i] // whole), spare)
            holding[i] = holding[i] + extra
            spare = spare - extra
    return np.array([reach] + holding)


def uneven(rng, amount, total, limit, lean):
    if amount == 2:
        one = jax.random.randint(rng, (), max(1, total - limit), min(limit, total - 1) + 1)
        return jnp.stack([one, total - one])
    sizes = jnp.asarray(split_up(amount, total, limit, lean), jnp.int32)
    couples = (amount - 1) // 2
    donor, sink = sizes[1:1 + 2 * couples:2], sizes[2:2 + 2 * couples:2]
    margin = jnp.minimum(donor - 1, limit - sink)
    shifted = jax.random.randint(jax.random.fold_in(rng, 1), (couples,), 0, 1 << 20) % (margin + 1)
    sizes = sizes.at[1:1 + 2 * couples:2].set(donor - shifted).at[2:2 + 2 * couples:2].set(sink + shifted)
    return sizes[jax.random.permutation(jax.random.fold_in(rng, 2), amount)]


def noise(own_key, extent, spread, most, split=(), kind=jnp.bfloat16):
    drawn = jax.random.normal(own_key, extent, jnp.float32) * spread
    if len(split) > 0:
        drawn = level_of(own_key, extent, split, -0.22, 0.18) * drawn
    return jnp.clip(drawn, min=-most, max=most).astype(kind)


def setup_inputs(seed: int = 0) -> dict:
    streams_of = jax.random.split(jax.random.key(seed), 11)
    return {
        "activations": noise(streams_of[0], (TOKENS, D), 1.0, 6.0, ((0, 8),)),
        "norm_gains": jnp.clip(1.0 + 0.18 * jax.random.normal(streams_of[1], (2, D), jnp.float32), 0.099609375, 1.8984375).astype(jnp.bfloat16),
        "w_query": noise(streams_of[2], (D, KV_HEADS, HEADS // KV_HEADS * HD), D ** -0.5, 0.125, ((0, 8), (1, 4))),
        "w_keyval": noise(streams_of[3], (D, KV_HEADS, 2 * HD), D ** -0.5, 0.125, ((0, 8), (1, 4))),
        "w_out": noise(streams_of[4], (KV_HEADS, HEADS // KV_HEADS * HD, D), 256 ** -0.5, 0.375, ((0, 4), (2, 8))),
        "w_gateup": noise(streams_of[5], (D, 2, FF), D ** -0.5, 0.125, ((0, 8), (2, 4))),
        "w_down": noise(streams_of[6], (FF, D), FF ** -0.5, 0.078125, ((0, 4), (1, 8))),
        "seq_lengths": uneven(streams_of[7], NSEQ, TOKENS, MAX_LEN, 2).astype(jnp.int32),
        "token_slot": draw_token_slot(jax.random.fold_in(streams_of[10], 71), 0),
        "out_grad": noise(streams_of[9], (TOKENS, D), 1.0, 6.0, ((0, 8),)),
    }


@jax.custom_vjp
def low(v):
    return lax.optimization_barrier(v.astype(jnp.bfloat16)).astype(jnp.float32)

@jax.custom_vjp
def low_back(v):
    return v

def low_keep(v):
    return (low(v), None)

def low_pass(kept, grad):
    return (grad,)

def back_keep(v):
    return (v, None)

def back_low(kept, grad):
    return (low(grad),)
low.defvjp(low_keep, low_pass)
low_back.defvjp(back_keep, back_low)
epsilon = 1e-05
rope_base = 10000.0
highest = lax.Precision.HIGHEST

def locate(seq_lengths, slot_values):
    seq_ends = jnp.cumsum(seq_lengths).astype(jnp.int32)
    seq_starts = (seq_ends - seq_lengths).astype(jnp.int32)
    inside = (slot_values[:, None] >= seq_starts[None, :]) & (slot_values[:, None] < seq_ends[None, :])
    first_slot = lax.optimization_barrier(jnp.sum(jnp.where(inside, seq_starts[None, :], 0), axis=1)).astype(jnp.int32)
    return (first_slot, (slot_values - first_slot).astype(jnp.int32))

def rotation(position):
    half_width = HD // 2
    frequency = rope_base ** (-jnp.arange(half_width, dtype=jnp.float32) * 2.0 / HD)
    angles = position.astype(jnp.float32)[:, None] * frequency[None, :]
    return (jnp.cos(angles), jnp.sin(angles))

def rotate(values, cosine_table, sine_table):
    half_width = values.shape[-1] // 2
    table_shape = (cosine_table.shape[0],) + (1,) * (values.ndim - 2) + (half_width,)
    cosine_part = cosine_table.reshape(table_shape)
    sine_part = sine_table.reshape(table_shape)
    first_half = values[..., :half_width]
    second_half = values[..., half_width:]
    return jnp.concatenate([first_half * cosine_part - second_half * sine_part, second_half * cosine_part + first_half * sine_part], axis=-1)

def normalize(values):
    return values * lax.rsqrt(lax.optimization_barrier(jnp.mean(values * values, axis=-1, keepdims=True)) + epsilon)

def divisor_rows(total_rows, row_limit):
    for candidate in range(min(total_rows, row_limit), 0, -1):
        if total_rows % candidate == 0:
            return candidate
    return 1

def reference(activations, norm_gains, w_query, w_keyval, w_out, w_gateup, w_down, seq_lengths, token_slot, out_grad):
    first_slot, position = locate(seq_lengths, jnp.arange(TOKENS, dtype=jnp.int32))
    cosine_table, sine_table = rotation(position)
    packed_acts = jnp.zeros((TOKENS, D), jnp.float32).at[token_slot].set(activations.astype(jnp.float32))
    packed_grad = jnp.zeros((TOKENS, D), jnp.float32).at[token_slot].set(out_grad.astype(jnp.float32))
    block_rows = divisor_rows(TOKENS, 512)
    groups = HEADS // KV_HEADS
    window = MAX_LEN + block_rows

    def forward(inputs, gains, query_w, keyval_w, out_w, gateup_w, down_w):
        lowered_one = low(normalize(inputs) * gains[0])
        query_lin = low_back(jnp.einsum('td,dhe->the', lowered_one, query_w, precision=highest))
        keyval_lin = low_back(jnp.einsum('td,dhe->the', lowered_one, keyval_w, precision=highest))
        queries = low(rotate(query_lin.reshape(TOKENS, KV_HEADS, groups, HD), cosine_table, sine_table))
        key_rows = low(rotate(keyval_lin[..., :HD], cosine_table, sine_table))
        value_rows = low(keyval_lin[..., HD:])
        padding = jnp.zeros((MAX_LEN, KV_HEADS, HD), jnp.float32)
        keys_padded = jnp.concatenate([padding, key_rows], axis=0)
        values_padded = jnp.concatenate([padding, value_rows], axis=0)

        def attend(block_start):
            query_block = lax.dynamic_slice_in_dim(queries, block_start, block_rows, 0)
            first_block = lax.dynamic_slice_in_dim(first_slot, block_start, block_rows, 0)
            key_block = lax.dynamic_slice_in_dim(keys_padded, block_start, window, 0)
            value_block = lax.dynamic_slice_in_dim(values_padded, block_start, window, 0)
            query_index = block_start + jnp.arange(block_rows, dtype=jnp.int32)
            key_index = block_start - MAX_LEN + jnp.arange(window, dtype=jnp.int32)
            allowed = (key_index[None, :] >= first_block[:, None]) & (key_index[None, :] <= query_index[:, None])
            scores = low_back(jnp.einsum('tgqd,kgd->tgqk', query_block, key_block, precision=highest) * 0.125)
            scores = jnp.where(allowed[:, None, None, :], scores, -1e+30)
            probs = jax.nn.softmax(scores, axis=-1)
            return jnp.einsum('tgqk,kgd->tgqd', low(probs), value_block, precision=highest)
        block_starts = (jnp.arange(TOKENS // block_rows, dtype=jnp.int32) * block_rows).astype(jnp.int32)
        attended = lax.map(jax.checkpoint(attend), block_starts).reshape(TOKENS, KV_HEADS, groups * HD)
        attended = low_back(attended)
        branch = low_back(jnp.einsum('the,hed->td', low(attended), out_w, precision=highest))
        middle = inputs + branch
        lowered_two = low(normalize(middle) * gains[1])
        gateup = low_back(jnp.einsum('td,dce->tce', lowered_two, gateup_w, precision=highest))
        hidden = low(jax.nn.silu(gateup[:, 0]) * gateup[:, 1])
        mixed = low_back(jnp.dot(hidden, down_w, precision=highest))
        return middle + mixed
    weights = [arr.astype(jnp.float32) for arr in (norm_gains, w_query, w_keyval, w_out, w_gateup, w_down)]
    outputs, pullback = jax.vjp(forward, packed_acts, *weights)
    grads = pullback(packed_grad)
    block_out = outputs[token_slot].astype(jnp.bfloat16)
    input_grad = grads[0][token_slot]
    return (block_out, input_grad, grads[1], grads[2], grads[3], grads[4], grads[5], grads[6])
```

```python
import jax
import jax.numpy as jnp
from jax import lax
from jax.sharding import PartitionSpec as P

HD = 64
SUB = 4


epsilon = 1e-05
rope_base = 10000.0
masked_fill = -1e30
low = jnp.bfloat16
wide = jnp.float32


def locate(seq_lengths, slot_values):
    seq_ends = jnp.cumsum(seq_lengths)
    seq_starts = seq_ends - seq_lengths
    inside = (slot_values[:, None] >= seq_starts[None, :]) & (
        slot_values[:, None] < seq_ends[None, :]
    )
    first_slot = jnp.sum(jnp.where(inside, seq_starts[None, :], 0), axis=1)
    return (first_slot, slot_values - first_slot)


def rotation(position):
    half_width = HD // 2
    frequency = rope_base ** (-jnp.arange(half_width, dtype=wide) * 2.0 / HD)
    angles = position.astype(wide)[:, None] * frequency[None, :]
    return (jnp.cos(angles), jnp.sin(angles))


def rotate(values, cosine_table, sine_table):
    half_width = values.shape[-1] // 2
    table_shape = (cosine_table.shape[0],) + (1,) * (values.ndim - 2) + (half_width,)
    cosine_part = cosine_table.reshape(table_shape)
    sine_part = sine_table.reshape(table_shape)
    first_half = values[..., :half_width]
    second_half = values[..., half_width:]
    return jnp.concatenate(
        [
            first_half * cosine_part - second_half * sine_part,
            second_half * cosine_part + first_half * sine_part,
        ],
        axis=-1,
    )


def scale_of(values):
    return lax.rsqrt(jnp.mean(values * values, axis=-1, keepdims=True) + epsilon)


def norm_back(scale, normed, incoming):
    return scale * (incoming - normed * jnp.mean(incoming * normed, axis=-1, keepdims=True))


def divisor_rows(total_rows, row_limit):
    for candidate in range(min(total_rows, row_limit), 0, -1):
        if total_rows % candidate == 0:
            return candidate
    return 1


def swap(x, axis, distance):
    size = lax.axis_size(axis)
    return lax.ppermute(x, axis, [(i, i ^ distance) for i in range(size)])


def to_all(x, axis):
    size = lax.axis_size(axis)
    copies = jnp.broadcast_to(x[None], (size,) + x.shape)
    return lax.all_to_all(copies, axis, 0, 0, tiled=True)


def heads_distances():
    distances = []
    step = lax.axis_size("heads") // 2
    while step >= 1:
        distances.append(step)
        step //= 2
    return distances


def heads_gather(x):
    for distance in heads_distances():
        x = jnp.concatenate([x, swap(x, "heads", distance)], axis=0)
    return x


def heads_sum_scatter(x):
    for distance in reversed(heads_distances()):
        half = x.shape[0] // 2
        x = x[:half] + swap(x[half:].astype(low), "heads", distance).astype(wide)
    return x


def sub_gather(x):
    teams = lax.axis_size("fsdp") // SUB
    return jnp.concatenate([x] + [swap(x, "fsdp", k * teams) for k in range(1, SUB)], axis=0)


def sub_sum_scatter(x):
    teams = lax.axis_size("fsdp") // SUB
    rows = x.shape[0] // SUB
    total = x[:rows]
    for k in range(1, SUB):
        total = total + swap(
            x[k * rows : (k + 1) * rows].astype(low), "fsdp", k * teams
        ).astype(wide)
    return total


def group_gather(x):
    return heads_gather(sub_gather(x))


def group_sum_scatter(x):
    return sub_sum_scatter(heads_sum_scatter(x))


def sub_exchange(x):
    devices = lax.axis_size("fsdp")
    teams = devices // SUB
    groups = [[g * teams + t for g in range(SUB)] for t in range(teams)]
    return lax.all_to_all(x, "fsdp", 0, 0, axis_index_groups=groups, tiled=True)


def on_device(
    activations,
    norm_gains,
    w_query,
    w_keyval,
    w_out,
    w_gateup,
    w_down,
    seq_lengths,
    token_slot,
    out_grad,
):
    devices = lax.axis_size("fsdp")
    head_devices = lax.axis_size("heads")
    teams = devices // SUB
    me_heads = lax.axis_index("heads")
    me_team = lax.axis_index("fsdp") % teams
    tok_rows = activations.shape[0]
    few = tok_rows // head_devices
    width = activations.shape[1]
    cols = width // devices
    groups = w_query.shape[2] // HD
    query_width = groups * HD
    units = w_down.shape[0]
    sub_units = units // SUB

    order = [0]
    for distance in heads_distances():
        order = order + [i ^ distance for i in order]

    def reorder(x):
        blocks = x.reshape((head_devices, few) + x.shape[1:])
        return jnp.concatenate(
            [lax.dynamic_index_in_dim(blocks, me_heads ^ i, 0, keepdims=False) for i in order],
            axis=0,
        )

    qkv_shard = jnp.concatenate([w_query[:, 0], w_keyval[:, 0]], axis=1)
    qkv_w = lax.all_gather(qkv_shard, "fsdp", axis=0, tiled=True)
    out_w = lax.all_gather(w_out[0], "fsdp", axis=1, tiled=True)

    activations = reorder(activations)
    out_grad = reorder(out_grad)
    token_slot = reorder(token_slot)

    small = jnp.concatenate([norm_gains.reshape(-1).astype(wide), token_slot.astype(wide)])
    small_all = to_all(small, "fsdp")
    gains = jnp.swapaxes(small_all[:, : 2 * cols].reshape(devices, 2, cols), 0, 1).reshape(2, width)
    slot_all = small_all[:, 2 * cols :].astype(jnp.int32).reshape(-1)

    gateup_parts = jnp.stack(
        [
            jnp.swapaxes(w_gateup[:, :, k * sub_units : (k + 1) * sub_units], 0, 1)
            for k in range(SUB)
        ],
        axis=0,
    )
    gateup_here = sub_exchange(gateup_parts)
    down_here = sub_exchange(w_down.reshape(SUB, sub_units, cols))
    upstream_group = group_gather(out_grad[:few])

    def all_teams(x):
        pieces = [x] + [swap(x, "fsdp", k) for k in range(1, teams)]
        if teams == 2:
            first = me_team == 0
            return jnp.stack(
                [jnp.where(first, pieces[0], pieces[1]), jnp.where(first, pieces[1], pieces[0])],
                axis=1,
            )
        table = jnp.stack(pieces, axis=1)
        return jnp.take(table, jnp.arange(teams) ^ me_team, axis=1)

    gateup_all = all_teams(gateup_here)
    down_all = all_teams(down_here)
    gate_w = gateup_all[:, :, 0].reshape(width, sub_units)
    up_w = gateup_all[:, :, 1].reshape(width, sub_units)
    gu_w = jnp.concatenate([gate_w, up_w], axis=1)
    down_w = jnp.moveaxis(down_all, 2, 0).reshape(sub_units, width)

    first_slot, position = locate(seq_lengths, token_slot)
    cosine_table, sine_table = rotation(position)
    inputs = activations.astype(wide)
    scale_one = scale_of(inputs)
    normed_one = inputs * scale_one
    lowered_one = (normed_one * gains[0]).astype(low)
    lowered_cols = lax.all_to_all(
        jnp.swapaxes(lowered_one.reshape(tok_rows, devices, cols), 0, 1),
        "fsdp",
        0,
        0,
        tiled=True,
    ).reshape(devices * tok_rows, cols)
    qkv_lin = jnp.dot(lowered_one, qkv_w, preferred_element_type=wide)
    queries = rotate(
        qkv_lin[:, :query_width].reshape(tok_rows, groups, HD), cosine_table, sine_table
    ).astype(low)
    key_rows = rotate(
        qkv_lin[:, query_width : query_width + HD], cosine_table, sine_table
    ).astype(low)
    keyvals = jnp.concatenate([key_rows, qkv_lin[:, query_width + HD :].astype(low)], axis=-1)
    key_all = to_all(keyvals, "fsdp").reshape(devices * tok_rows, 2 * HD)
    total_keys = key_all.shape[0]
    block_rows = divisor_rows(total_keys, 1024)
    key_blocks = (
        key_all.reshape(total_keys // block_rows, block_rows, 2 * HD),
        slot_all.reshape(total_keys // block_rows, block_rows),
    )
    slot_column = token_slot[:, None]
    first_column = first_slot[:, None]

    def scores_of(key_block, slot_block):
        logits = (
            jnp.einsum("tqd,kd->tqk", queries, key_block, preferred_element_type=wide) * 0.125
        )
        allowed = (slot_block[None, :] <= slot_column) & (slot_block[None, :] >= first_column)
        return (logits, allowed[:, None, :])

    def absorb(running, blocks):
        running_max, running_sum, running_out = running
        key_block, slot_block = blocks
        logits, allowed = scores_of(key_block[:, :HD], slot_block)
        newest = jnp.maximum(running_max, jnp.max(jnp.where(allowed, logits, masked_fill), axis=-1))
        weights = jnp.where(allowed, jnp.exp(logits - newest[..., None]), 0.0)
        factor = jnp.exp(running_max - newest)
        running_sum = running_sum * factor + jnp.sum(weights, axis=-1)
        running_out = running_out * factor[..., None] + jnp.einsum(
            "tqk,kd->tqd", weights.astype(low), key_block[:, HD:], preferred_element_type=wide
        )
        return ((newest, running_sum, running_out), None)

    start_state = (
        jnp.full((tok_rows, groups), masked_fill, wide),
        jnp.zeros((tok_rows, groups), wide),
        jnp.zeros((tok_rows, groups, HD), wide),
    )
    (final_max, final_sum, final_out), unused = lax.scan(absorb, start_state, key_blocks)
    attended = final_out / final_sum[..., None]
    log_total = final_max + jnp.log(final_sum)
    attended_low = attended.reshape(tok_rows, query_width).astype(low)
    branch = heads_sum_scatter(jnp.dot(attended_low, out_w, preferred_element_type=wide))
    attended_all = to_all(attended_low, "fsdp").reshape(devices * tok_rows, query_width)

    middle = inputs[:few] + branch
    scale_two = scale_of(middle)
    normed_two = middle * scale_two
    lowered_two = (normed_two * gains[1]).astype(low)
    lowered_group = group_gather(lowered_two)
    hidden_grad = lax.dot_general(
        upstream_group, down_w, (((1,), (1,)), ((), ())), preferred_element_type=wide
    )
    gateup = jnp.dot(lowered_group, gu_w, preferred_element_type=wide)
    gate_pre = gateup[:, :sub_units]
    up_pre = gateup[:, sub_units:]
    sigmoid_gate = jax.nn.sigmoid(gate_pre)
    activated = gate_pre * sigmoid_gate
    hidden = (activated * up_pre).astype(low)
    gate_grad = hidden_grad * up_pre * sigmoid_gate * (1.0 + gate_pre * (1.0 - sigmoid_gate))
    up_grad = hidden_grad * activated
    gu_grad = jnp.concatenate([gate_grad, up_grad], axis=1).astype(low)
    lowered_grad_two = group_sum_scatter(
        lax.dot_general(gu_grad, gu_w, (((1,), (1,)), ((), ())), preferred_element_type=wide)
    )
    gain_grad_two = jnp.sum(lowered_grad_two * normed_two, axis=0)
    middle_grad = out_grad[:few].astype(wide) + norm_back(
        scale_two, normed_two, lowered_grad_two * gains[1]
    )
    branch_grad = heads_gather(middle_grad.astype(low))

    mixed = group_sum_scatter(jnp.dot(hidden, down_w, preferred_element_type=wide))
    block_out = lax.all_gather((middle + mixed).astype(low), "heads", axis=0, tiled=True)

    def teams_sum(make):
        total = make(me_team)
        for k in range(1, teams):
            total = total + swap(make(me_team ^ k).astype(low), "fsdp", k).astype(wide)
        return total

    def team_columns(x, team):
        blocks = x.reshape(x.shape[0], SUB, teams, cols)
        return lax.dynamic_index_in_dim(blocks, team, 2, keepdims=False).reshape(-1, SUB * cols)

    def gateup_term(team):
        term = lax.dot_general(
            team_columns(lowered_group, team),
            gu_grad,
            (((0,), (0,)), ((), ())),
            preferred_element_type=wide,
        )
        return term.reshape(SUB, cols, 2 * sub_units)

    def down_term(team):
        term = lax.dot_general(
            hidden,
            team_columns(upstream_group, team),
            (((0,), (0,)), ((), ())),
            preferred_element_type=wide,
        )
        return jnp.swapaxes(term.reshape(sub_units, SUB, cols), 0, 1)

    gateup_owned = sub_exchange(teams_sum(gateup_term).astype(low))
    gateup_owned = jnp.concatenate(
        [
            jnp.concatenate([gateup_owned[k, :, c * sub_units : (c + 1) * sub_units] for k in range(SUB)], axis=1)[
                :, None
            ]
            for c in range(2)
        ],
        axis=1,
    ).astype(wide)
    down_owned = sub_exchange(teams_sum(down_term).astype(low)).reshape(units, cols).astype(wide)

    branch_cols = lax.all_to_all(
        jnp.swapaxes(branch_grad.reshape(tok_rows, devices, cols), 0, 1),
        "fsdp",
        0,
        0,
        tiled=True,
    ).reshape(devices * tok_rows, cols)
    out_owned = lax.dot_general(
        attended_all, branch_cols, (((0,), (0,)), ((), ())), preferred_element_type=wide
    )[None]

    attended_grad = lax.dot_general(
        branch_grad, out_w, (((1,), (1,)), ((), ())), preferred_element_type=wide
    )
    attended_grad = attended_grad.reshape(tok_rows, groups, HD).astype(low)
    delta = jnp.sum(attended_grad.astype(wide) * attended, axis=-1)

    def backstep(query_grad, blocks):
        key_block, slot_block = blocks
        logits, allowed = scores_of(key_block[:, :HD], slot_block)
        probs = jnp.where(allowed, jnp.exp(logits - log_total[..., None]), 0.0)
        value_grad = jnp.einsum(
            "tqk,tqd->kd", probs.astype(low), attended_grad, preferred_element_type=wide
        )
        prob_grad = jnp.einsum(
            "tqd,kd->tqk", attended_grad, key_block[:, HD:], preferred_element_type=wide
        )
        score_grad = (probs * (prob_grad - delta[..., None])).astype(low)
        query_grad = query_grad + 0.125 * jnp.einsum(
            "tqk,kd->tqd", score_grad, key_block[:, :HD], preferred_element_type=wide
        )
        key_grad = 0.125 * jnp.einsum(
            "tqk,tqd->kd", score_grad, queries, preferred_element_type=wide
        )
        return (query_grad, jnp.concatenate([key_grad, value_grad], axis=-1))

    query_grad, keyval_terms = lax.scan(
        backstep, jnp.zeros((tok_rows, groups, HD), wide), key_blocks
    )
    keyval_pieces = lax.all_to_all(
        keyval_terms.reshape(devices, tok_rows, 2 * HD).astype(low), "fsdp", 0, 0, tiled=True
    )
    keyval_sum = jnp.sum(keyval_pieces.astype(wide), axis=0)
    key_unrotated = rotate(keyval_sum[:, :HD], cosine_table, -sine_table)
    keyval_grad = jnp.concatenate([key_unrotated, keyval_sum[:, HD:]], axis=-1).astype(low)
    query_lin_grad = (
        rotate(query_grad, cosine_table, -sine_table).reshape(tok_rows, query_width).astype(low)
    )
    qkv_grad = jnp.concatenate([query_lin_grad, keyval_grad], axis=1)
    lowered_part = lax.dot_general(
        qkv_grad, qkv_w, (((1,), (1,)), ((), ())), preferred_element_type=wide
    )
    gain_grad_one = jnp.sum(lowered_part * normed_one, axis=0)
    lowered_grad_one = heads_sum_scatter(lowered_part)
    input_grad = middle_grad + norm_back(
        scale_one[:few], normed_one[:few], lowered_grad_one * gains[0]
    )
    input_grad = lax.all_gather(input_grad.astype(low), "heads", axis=0, tiled=True).astype(wide)

    gain_terms = jnp.stack([gain_grad_one, gain_grad_two], axis=0)
    gain_pieces = lax.all_to_all(
        jnp.swapaxes(gain_terms.reshape(2, devices, cols), 0, 1), "fsdp", 0, 0, tiled=True
    )
    gains_owned = jnp.sum(gain_pieces, axis=0)
    for distance in heads_distances():
        gains_owned = gains_owned + swap(gains_owned, "heads", distance)

    query_all = to_all(query_lin_grad, "fsdp").reshape(devices * tok_rows, query_width)
    keyval_all = to_all(keyval_grad, "fsdp").reshape(devices * tok_rows, 2 * HD)
    query_owned = lax.dot_general(
        lowered_cols, query_all, (((0,), (0,)), ((), ())), preferred_element_type=wide
    )[:, None]
    keyval_owned = lax.dot_general(
        lowered_cols, keyval_all, (((0,), (0,)), ((), ())), preferred_element_type=wide
    )[:, None]
    return (
        block_out,
        input_grad,
        gains_owned,
        query_owned,
        keyval_owned,
        out_owned,
        gateup_owned,
        down_owned,
    )


def solution(mesh):
    placed = (
        P("fsdp", None),
        P(None, "fsdp"),
        P("fsdp", "heads", None),
        P("fsdp", "heads", None),
        P("heads", None, "fsdp"),
        P("fsdp", None, "heads"),
        P("heads", "fsdp"),
        P(),
        P("fsdp"),
        P("fsdp", None),
    )
    return jax.shard_map(
        on_device,
        mesh=mesh,
        in_specs=placed,
        out_specs=(
            P("fsdp", None),
            P("fsdp", None),
            P(None, "fsdp"),
            P("fsdp", "heads", None),
            P("fsdp", "heads", None),
            P("heads", None, "fsdp"),
            P("fsdp", None, "heads"),
            P("heads", "fsdp"),
        ),
        check_vma=False,
    )
```

```python
import jax
import jax.numpy as jnp
from jax import lax
from jax.sharding import PartitionSpec as P

HD = 64
SUB = 4


epsilon = 1e-05
rope_base = 10000.0
masked_fill = -1e30
low = jnp.bfloat16
wide = jnp.float32


def locate(seq_lengths, slot_values):
    seq_ends = jnp.cumsum(seq_lengths)
    seq_starts = seq_ends - seq_lengths
    inside = (slot_values[:, None] >= seq_starts[None, :]) & (
        slot_values[:, None] < seq_ends[None, :]
    )
    first_slot = jnp.sum(jnp.where(inside, seq_starts[None, :], 0), axis=1)
    return (first_slot, slot_values - first_slot)


def rotation(position):
    half_width = HD // 2
    frequency = rope_base ** (-jnp.arange(half_width, dtype=wide) * 2.0 / HD)
    angles = position.astype(wide)[:, None] * frequency[None, :]
    return (jnp.cos(angles), jnp.sin(angles))


def rotate(values, cosine_table, sine_table):
    half_width = values.shape[-1] // 2
    table_shape = (cosine_table.shape[0],) + (1,) * (values.ndim - 2) + (half_width,)
    cosine_part = cosine_table.reshape(table_shape)
    sine_part = sine_table.reshape(table_shape)
    first_half = values[..., :half_width]
    second_half = values[..., half_width:]
    return jnp.concatenate(
        [
            first_half * cosine_part - second_half * sine_part,
            second_half * cosine_part + first_half * sine_part,
        ],
        axis=-1,
    )


def scale_of(values):
    return lax.rsqrt(jnp.mean(values * values, axis=-1, keepdims=True) + epsilon)


def norm_back(scale, normed, incoming):
    return scale * (incoming - normed * jnp.mean(incoming * normed, axis=-1, keepdims=True))


def divisor_rows(total_rows, row_limit):
    for candidate in range(min(total_rows, row_limit), 0, -1):
        if total_rows % candidate == 0:
            return candidate
    return 1


def swap(x, axis, distance):
    size = lax.axis_size(axis)
    return lax.ppermute(x, axis, [(i, i ^ distance) for i in range(size)])


def after(x, *others):
    return lax.optimization_barrier((x,) + others)[0]


def to_all(x, axis):
    size = lax.axis_size(axis)
    copies = jnp.broadcast_to(x[None], (size,) + x.shape)
    return lax.all_to_all(copies, axis, 0, 0, tiled=True)


def heads_distances():
    distances = []
    step = lax.axis_size("heads") // 2
    while step >= 1:
        distances.append(step)
        step //= 2
    return distances


def sub_distances():
    teams = lax.axis_size("fsdp") // SUB
    return [k * teams for k in range(1, SUB)]


def sub_gather(x):
    return jnp.concatenate([x] + [swap(x, "fsdp", d) for d in sub_distances()], axis=0)


def heads_gather(x, earlier=()):
    *others, last = heads_distances()
    for distance in others:
        x = jnp.concatenate([x, swap(x, "heads", distance)], axis=0)
    if earlier:
        x = after(x, *earlier)
    return jnp.concatenate([x, swap(x, "heads", last)], axis=0)


def group_gather(x, earlier=()):
    x = sub_gather(x)
    if earlier:
        x = after(x, *earlier)
    return heads_gather(x)


def group_blocks():
    blocks = [(k, 0) for k in range(SUB)]
    for distance in heads_distances():
        blocks = blocks + [(k, d ^ distance) for k, d in blocks]
    return blocks


def first_sum(make, rows):
    half = rows // 2
    distance = heads_distances()[-1]
    away = swap(make(half, rows).astype(low), "heads", distance)
    return make(0, half) + away.astype(wide)


def other_sums(x):
    for distance in reversed(heads_distances()[:-1]):
        half = x.shape[0] // 2
        x = x[:half] + swap(x[half:].astype(low), "heads", distance).astype(wide)
    return x


def sub_sum(x):
    few = x.shape[0] // SUB
    total = x[:few]
    for k, distance in enumerate(sub_distances()):
        away = swap(x[(k + 1) * few : (k + 2) * few].astype(low), "fsdp", distance)
        total = total + away.astype(wide)
    return total


def sub_exchange(x):
    devices = lax.axis_size("fsdp")
    teams = devices // SUB
    groups = [[g * teams + t for g in range(SUB)] for t in range(teams)]
    return lax.all_to_all(x, "fsdp", 0, 0, axis_index_groups=groups, tiled=True)


def teams_pieces(x):
    teams = lax.axis_size("fsdp") // SUB
    return [x] + [swap(x, "fsdp", k) for k in range(1, teams)]


def own_team_first(x):
    teams = lax.axis_size("fsdp") // SUB
    me_team = lax.axis_index("fsdp") % teams
    blocks = x.reshape(x.shape[0], SUB, teams, -1)
    if teams == 2:
        first, second = (blocks[:, :, t].reshape(x.shape[0], -1) for t in range(2))
        swapped = me_team == 1
        return jnp.concatenate(
            [jnp.where(swapped, second, first), jnp.where(swapped, first, second)], axis=1
        )
    blocks = jnp.take(blocks, jnp.arange(teams) ^ me_team, axis=2)
    return jnp.swapaxes(blocks, 1, 2).reshape(x.shape)


def teams_in_place(x):
    teams = lax.axis_size("fsdp") // SUB
    me_team = lax.axis_index("fsdp") % teams
    blocks = x.reshape(x.shape[0], teams, SUB, -1)
    if teams == 2:
        swapped = me_team == 1
        pair = [
            jnp.where(swapped, blocks[:, 1], blocks[:, 0]),
            jnp.where(swapped, blocks[:, 0], blocks[:, 1]),
        ]
        return jnp.stack(pair, axis=2).reshape(x.shape)
    blocks = jnp.take(blocks, jnp.arange(teams) ^ me_team, axis=1)
    return jnp.swapaxes(blocks, 1, 2).reshape(x.shape)


def teams_sum(make):
    teams = lax.axis_size("fsdp") // SUB
    away = [swap(make(k).astype(low), "fsdp", k) for k in range(1, teams)]
    total = make(0)
    for piece in away:
        total = total + piece.astype(wide)
    return total.astype(low)


def wider(x, size, axis):
    missing = [(0, 0)] * x.ndim
    missing[axis] = (0, size - x.shape[axis])
    return jnp.pad(x, missing)


def over_rows(left, right):
    return lax.dot_general(left, right, (((0,), (0,)), ((), ())), preferred_element_type=wide)


def over_cols(left, right):
    return lax.dot_general(left, right, (((1,), (1,)), ((), ())), preferred_element_type=wide)


def on_device(
    activations,
    norm_gains,
    w_query,
    w_keyval,
    w_out,
    w_gateup,
    w_down,
    seq_lengths,
    token_slot,
    out_grad,
):
    devices = lax.axis_size("fsdp")
    head_devices = lax.axis_size("heads")
    teams = devices // SUB
    me_heads = lax.axis_index("heads")
    me_team = lax.axis_index("fsdp") % teams
    me_sub = lax.axis_index("fsdp") // teams
    tok_rows, width = activations.shape
    few = tok_rows // head_devices
    rows = SUB * tok_rows
    cols = width // devices
    groups = w_query.shape[2] // HD // SUB
    query_width = groups * HD
    units = w_down.shape[0]
    sub_units = -(-units // (SUB * 128)) * 128
    qkv_width = query_width + 2 * HD
    lanes = max(qkv_width, cols)
    team_width = SUB * cols

    def share(x):
        return lax.dynamic_slice_in_dim(x, me_heads * few, few, 0)

    x_sub = sub_gather(own_team_first(share(activations)))

    extras = jnp.concatenate(
        [
            wider(norm_gains, lanes, 1),
            wider((token_slot // 128).astype(low)[None], lanes, 1),
            wider((token_slot % 128).astype(low)[None], lanes, 1),
            jnp.zeros((12, lanes), low),
        ],
        axis=0,
    )
    extras = lax.optimization_barrier(extras)
    attention_parts = jnp.stack(
        [
            jnp.concatenate(
                [
                    wider(
                        jnp.concatenate(
                            [
                                w_query[:, 0, k * query_width : (k + 1) * query_width],
                                w_keyval[:, 0],
                            ],
                            axis=1,
                        ),
                        lanes,
                        1,
                    ),
                    extras,
                ],
                axis=0,
            )
            for k in range(SUB)
        ],
        axis=0,
    )
    attention_here = sub_exchange(attention_parts)
    attention_pieces = teams_pieces(attention_here)
    x_group = heads_gather(x_sub, (attention_here,))
    qkv_w = jnp.concatenate(
        [piece[:, :cols, :qkv_width].reshape(team_width, qkv_width) for piece in attention_pieces],
        axis=0,
    )
    extras_all = jnp.stack([piece[:, cols:] for piece in attention_pieces], axis=0)
    gains = jnp.swapaxes(extras_all[:, :, :2, :cols].reshape(devices, 2, cols), 0, 1)
    gains = gains.reshape(2, width).astype(wide)
    slot_parts = extras_all[:, :, 2:4, :tok_rows].astype(jnp.int32)
    slot_blocks = (slot_parts[:, :, 0] * 128 + slot_parts[:, :, 1]).reshape(
        devices * head_devices, few
    )
    block_places = [
        ((t * SUB + (me_sub ^ k)) * head_devices) + (me_heads ^ d)
        for t in range(teams)
        for k, d in group_blocks()
    ]
    slot_all = jnp.take(slot_blocks, jnp.stack(block_places), axis=0).reshape(teams * rows)
    slot_group = slot_all[:rows]

    tall_parts = jnp.concatenate(
        [
            w_out[0].reshape(SUB, query_width, cols),
            wider(w_down, SUB * sub_units, 0).reshape(SUB, sub_units, cols),
        ],
        axis=1,
    )
    tall_here = sub_exchange(after(tall_parts, attention_here))
    tall_pieces = teams_pieces(tall_here)
    out_w = jnp.concatenate(
        [piece[z, :query_width] for piece in tall_pieces for z in range(SUB)], axis=1
    )
    down_w = jnp.concatenate(
        [piece[z, query_width:] for piece in tall_pieces for z in range(SUB)], axis=1
    )
    gateup_parts = wider(w_gateup, SUB * sub_units, 2)
    gateup_parts = jnp.stack(
        [
            jnp.concatenate(
                [gateup_parts[:, c, k * sub_units : (k + 1) * sub_units] for c in range(2)], axis=1
            )
            for k in range(SUB)
        ],
        axis=0,
    )
    gateup_here = sub_exchange(after(gateup_parts, tall_here))
    half_sub = SUB // 2
    gateup_halves = [
        [swap(part, "fsdp", k) for k in range(1, teams)]
        for part in (gateup_here[:half_sub], gateup_here[half_sub:])
    ]
    gateup_pieces = [gateup_here] + [jnp.concatenate(pair, axis=0) for pair in zip(*gateup_halves)]
    upstream_share = own_team_first(share(out_grad))
    upstream_sub = sub_gather(after(upstream_share, x_sub))
    upstream_group = heads_gather(upstream_sub)

    first_slot, position = locate(seq_lengths, slot_group)
    cosine_table, sine_table = rotation(position)
    inputs = x_group.astype(wide)
    scale_one = scale_of(inputs)
    normed_one = inputs * scale_one
    lowered_one = after((normed_one * gains[0]).astype(low), x_group)
    qkv_lin = jnp.dot(lowered_one, qkv_w, preferred_element_type=wide)
    queries = rotate(
        qkv_lin[:, :query_width].reshape(rows, groups, HD), cosine_table, sine_table
    ).astype(low)
    queries = after(queries, tall_here, upstream_sub)
    key_rows = rotate(
        qkv_lin[:, query_width : query_width + HD], cosine_table, sine_table
    ).astype(low)
    keyvals = jnp.concatenate([key_rows, qkv_lin[:, query_width + HD :].astype(low)], axis=-1)
    key_all = jnp.concatenate(
        [keyvals] + [swap(keyvals, "fsdp", k) for k in range(1, teams)], axis=0
    )
    total_keys = key_all.shape[0]
    block_rows = divisor_rows(total_keys, 1024)
    key_blocks = (
        key_all.reshape(total_keys // block_rows, block_rows, 2 * HD),
        slot_all.reshape(total_keys // block_rows, block_rows),
    )
    slot_column = slot_group[:, None]
    first_column = first_slot[:, None]

    def scores_of(key_block, slot_block):
        logits = (
            jnp.einsum("tqd,kd->tqk", queries, key_block, preferred_element_type=wide) * 0.125
        )
        allowed = (slot_block[None, :] <= slot_column) & (slot_block[None, :] >= first_column)
        return (logits, allowed[:, None, :])

    def absorb(running, blocks):
        running_max, running_sum, running_out = running
        key_block, slot_block = blocks
        logits, allowed = scores_of(key_block[:, :HD], slot_block)
        newest = jnp.maximum(running_max, jnp.max(jnp.where(allowed, logits, masked_fill), axis=-1))
        weights = jnp.where(allowed, jnp.exp(logits - newest[..., None]), 0.0)
        factor = jnp.exp(running_max - newest)
        running_sum = running_sum * factor + jnp.sum(weights, axis=-1)
        running_out = running_out * factor[..., None] + jnp.einsum(
            "tqk,kd->tqd", weights.astype(low), key_block[:, HD:], preferred_element_type=wide
        )
        return ((newest, running_sum, running_out), None)

    start_state = (
        jnp.full((rows, groups), masked_fill, wide),
        jnp.zeros((rows, groups), wide),
        jnp.zeros((rows, groups, HD), wide),
    )
    (final_max, final_sum, final_out), unused = lax.scan(absorb, start_state, key_blocks)
    attended = final_out / final_sum[..., None]
    log_total = final_max + jnp.log(final_sum)
    attended_low = attended.reshape(rows, query_width).astype(low)
    attended_low = after(attended_low, upstream_group)
    branch = first_sum(
        lambda first, end: jnp.dot(attended_low[first:end], out_w, preferred_element_type=wide),
        rows,
    )
    branch = other_sums(after(branch, gateup_here))
    branch = sub_sum(after(branch, *gateup_halves[0]))

    middle = inputs[:few] + branch
    scale_two = scale_of(middle)
    normed_two = middle * scale_two
    gu_w = jnp.concatenate(
        [piece.reshape(team_width, 2 * sub_units) for piece in gateup_pieces], axis=0
    )
    lowered_sub = sub_gather((normed_two * gains[1]).astype(low))
    lowered_group = heads_gather(after(lowered_sub, *gateup_halves[1]))
    hidden_grad = over_cols(upstream_group, down_w)
    gateup = jnp.dot(lowered_group, gu_w, preferred_element_type=wide)
    gate_pre = gateup[:, :sub_units]
    up_pre = gateup[:, sub_units:]
    sigmoid_gate = jax.nn.sigmoid(gate_pre)
    activated = gate_pre * sigmoid_gate
    hidden = (activated * up_pre).astype(low)
    gate_grad = hidden_grad * up_pre * sigmoid_gate * (1.0 + gate_pre * (1.0 - sigmoid_gate))
    up_grad = hidden_grad * activated
    gu_grad = jnp.concatenate([gate_grad, up_grad], axis=1).astype(low)
    lowered_grad_two = sub_sum(
        other_sums(first_sum(lambda first, end: over_cols(gu_grad[first:end], gu_w), rows))
    )
    gain_grad_two = jnp.sum(lowered_grad_two * normed_two, axis=0)
    middle_grad = upstream_share.astype(wide) + norm_back(
        scale_two, normed_two, lowered_grad_two * gains[1]
    )
    def team_cols(x, k):
        return x[:, k * team_width : (k + 1) * team_width]

    def gateup_term(k):
        return over_rows(team_cols(lowered_group, k), gu_grad).reshape(SUB, cols, 2 * sub_units)

    def down_term(k):
        term = over_rows(hidden, team_cols(upstream_group, k))
        return jnp.moveaxis(term.reshape(sub_units, SUB, cols), 1, 0)

    gateup_sum = teams_sum(gateup_term)
    down_sum = teams_sum(down_term)
    branch_sub = sub_gather(after(middle_grad.astype(low), gateup_sum))
    branch_grad = heads_gather(branch_sub)
    gateup_owned = sub_exchange(after(gateup_sum, branch_sub))
    down_owned = sub_exchange(after(down_sum, gateup_owned))
    mixed = sub_sum(
        other_sums(
            first_sum(
                lambda first, end: jnp.dot(
                    after(hidden, branch_grad)[first:end], down_w, preferred_element_type=wide
                ),
                rows,
            )
        )
    )
    block_out = teams_in_place((middle + mixed).astype(low))
    block_out = lax.all_gather(block_out, "heads", axis=0, tiled=True)

    attended_grad = over_cols(branch_grad, out_w).reshape(rows, groups, HD).astype(low)
    delta = jnp.sum(attended_grad.astype(wide) * attended, axis=-1)

    def backstep(query_grad, blocks):
        key_block, slot_block = blocks
        logits, allowed = scores_of(key_block[:, :HD], slot_block)
        probs = jnp.where(allowed, jnp.exp(logits - log_total[..., None]), 0.0)
        value_grad = jnp.einsum(
            "tqk,tqd->kd", probs.astype(low), attended_grad, preferred_element_type=wide
        )
        prob_grad = jnp.einsum(
            "tqd,kd->tqk", attended_grad, key_block[:, HD:], preferred_element_type=wide
        )
        score_grad = (probs * (prob_grad - delta[..., None])).astype(low)
        query_grad = query_grad + 0.125 * jnp.einsum(
            "tqk,kd->tqd", score_grad, key_block[:, :HD], preferred_element_type=wide
        )
        key_grad = 0.125 * jnp.einsum(
            "tqk,tqd->kd", score_grad, queries, preferred_element_type=wide
        )
        return (query_grad, jnp.concatenate([key_grad, value_grad], axis=-1))

    query_grad, keyval_terms = lax.scan(
        backstep, jnp.zeros((rows, groups, HD), wide), key_blocks
    )
    keyval_terms = keyval_terms.reshape(teams, rows, 2 * HD)
    keyval_sum = keyval_terms[0]
    for k in range(1, teams):
        keyval_sum = keyval_sum + swap(keyval_terms[k].astype(low), "fsdp", k).astype(wide)
    key_unrotated = rotate(keyval_sum[:, :HD], cosine_table, -sine_table)
    query_unrotated = rotate(query_grad, cosine_table, -sine_table).reshape(rows, query_width)
    qkv_grad = jnp.concatenate(
        [query_unrotated, key_unrotated, keyval_sum[:, HD:]], axis=-1
    ).astype(low)
    qkv_grad = after(qkv_grad, gateup_owned, down_sum)
    half_grad_one = first_sum(lambda first, end: over_cols(qkv_grad[first:end], qkv_w), rows)
    lowered_grad_one = sub_sum(after(other_sums(half_grad_one), down_owned))
    input_grad = middle_grad + norm_back(
        scale_one[:few], normed_one[:few], lowered_grad_one * gains[0]
    )
    input_grad = after(teams_in_place(input_grad.astype(low)), block_out)
    input_grad = lax.all_gather(input_grad, "heads", axis=0, tiled=True).astype(wide)

    def attention_term(k):
        late_grad = after(qkv_grad, half_grad_one) if k == 0 else qkv_grad
        qkv_term = over_rows(team_cols(lowered_one, k), late_grad)
        gain_term = jnp.sum(
            qkv_term * qkv_w[k * team_width : (k + 1) * team_width].astype(wide), axis=1
        ).reshape(SUB, 1, cols)
        gain_two_term = gain_grad_two[k * team_width : (k + 1) * team_width].reshape(SUB, 1, cols)
        gain_terms = jnp.concatenate([gain_term, gain_two_term], axis=1)
        out_term = over_rows(attended_low, team_cols(branch_grad, k))
        out_term = jnp.moveaxis(out_term.reshape(query_width, SUB, cols), 1, 0)
        return jnp.concatenate(
            [
                wider(qkv_term.reshape(SUB, cols, qkv_width), lanes, 2),
                wider(out_term, lanes, 2),
                wider(wider(gain_terms, lanes, 2), 16, 1),
            ],
            axis=1,
        )

    attention_owned = sub_exchange(after(teams_sum(attention_term), down_owned)).astype(wide)
    query_owned = jnp.concatenate(
        [attention_owned[k, :cols, :query_width] for k in range(SUB)], axis=1
    )[:, None]
    keyval_owned = jnp.sum(attention_owned[:, :cols, query_width:qkv_width], axis=0)[:, None]
    out_owned = attention_owned[:, cols : cols + query_width, :cols].reshape(
        1, SUB * query_width, cols
    )
    gains_owned = jnp.sum(
        attention_owned[:, cols + query_width : cols + query_width + 2, :cols], axis=0
    )
    for distance in heads_distances():
        gains_owned = gains_owned + swap(gains_owned, "heads", distance)
    gains_owned = jnp.stack([gains_owned[0] / norm_gains[0].astype(wide), gains_owned[1]], axis=0)
    gateup_owned = jnp.stack(
        [
            jnp.concatenate(
                [gateup_owned[k, :cols, c * sub_units : (c + 1) * sub_units] for k in range(SUB)],
                axis=1,
            )[:, :units]
            for c in range(2)
        ],
        axis=1,
    ).astype(wide)
    down_owned = down_owned.reshape(SUB * sub_units, cols)[:units].astype(wide)
    return (
        block_out,
        input_grad,
        gains_owned,
        query_owned,
        keyval_owned,
        out_owned,
        gateup_owned,
        down_owned,
    )


def solution(mesh):
    placed = (
        P("fsdp", None),
        P(None, "fsdp"),
        P("fsdp", "heads", None),
        P("fsdp", "heads", None),
        P("heads", None, "fsdp"),
        P("fsdp", None, "heads"),
        P("heads", "fsdp"),
        P(),
        P("fsdp"),
        P("fsdp", None),
    )
    return jax.shard_map(
        on_device,
        mesh=mesh,
        in_specs=placed,
        out_specs=(
            P("fsdp", None),
            P("fsdp", None),
            P(None, "fsdp"),
            P("fsdp", "heads", None),
            P("fsdp", "heads", None),
            P("heads", None, "fsdp"),
            P("fsdp", None, "heads"),
            P("heads", "fsdp"),
        ),
        check_vma=False,
    )
```

```python
import jax
import jax.numpy as jnp
from jax import lax
from jax.sharding import PartitionSpec as P

HD = 64
SUB = 4


epsilon = 1e-05
rope_base = 10000.0
masked_fill = -1e30
low = jnp.bfloat16
wide = jnp.float32


def locate(seq_lengths, slot_values):
    seq_ends = jnp.cumsum(seq_lengths)
    seq_starts = seq_ends - seq_lengths
    inside = (slot_values[:, None] >= seq_starts[None, :]) & (
        slot_values[:, None] < seq_ends[None, :]
    )
    first_slot = jnp.sum(jnp.where(inside, seq_starts[None, :], 0), axis=1)
    return (first_slot, slot_values - first_slot)


def rotation(position):
    half_width = HD // 2
    frequency = rope_base ** (-jnp.arange(half_width, dtype=wide) * 2.0 / HD)
    angles = position.astype(wide)[:, None] * frequency[None, :]
    return (jnp.cos(angles), jnp.sin(angles))


def rotate(values, cosine_table, sine_table):
    half_width = values.shape[-1] // 2
    table_shape = (cosine_table.shape[0],) + (1,) * (values.ndim - 2) + (half_width,)
    cosine_part = cosine_table.reshape(table_shape)
    sine_part = sine_table.reshape(table_shape)
    first_half = values[..., :half_width]
    second_half = values[..., half_width:]
    return jnp.concatenate(
        [
            first_half * cosine_part - second_half * sine_part,
            second_half * cosine_part + first_half * sine_part,
        ],
        axis=-1,
    )


def scale_of(values):
    return lax.rsqrt(jnp.mean(values * values, axis=-1, keepdims=True) + epsilon)


def norm_back(scale, normed, incoming):
    return scale * (incoming - normed * jnp.mean(incoming * normed, axis=-1, keepdims=True))


def divisor_rows(total_rows, row_limit):
    for candidate in range(min(total_rows, row_limit), 0, -1):
        if total_rows % candidate == 0:
            return candidate
    return 1


def swap(x, axis, distance):
    size = lax.axis_size(axis)
    return lax.ppermute(x, axis, [(i, i ^ distance) for i in range(size)])


def after(x, *others):
    return lax.optimization_barrier((x,) + others)[0]


def to_all(x, axis):
    size = lax.axis_size(axis)
    copies = jnp.broadcast_to(x[None], (size,) + x.shape)
    return lax.all_to_all(copies, axis, 0, 0, tiled=True)


def heads_distances():
    distances = []
    step = lax.axis_size("heads") // 2
    while step >= 1:
        distances.append(step)
        step //= 2
    return distances


def sub_distances():
    teams = lax.axis_size("fsdp") // SUB
    return [k * teams for k in range(1, SUB)]


def sub_gather(x):
    return jnp.concatenate([x] + [swap(x, "fsdp", d) for d in sub_distances()], axis=0)


def heads_gather(x, earlier=()):
    *others, last = heads_distances()
    for distance in others:
        x = jnp.concatenate([x, swap(x, "heads", distance)], axis=0)
    if earlier:
        x = after(x, *earlier)
    return jnp.concatenate([x, swap(x, "heads", last)], axis=0)


def group_gather(x, earlier=()):
    x = sub_gather(x)
    if earlier:
        x = after(x, *earlier)
    return heads_gather(x)


def group_blocks():
    blocks = [(k, 0) for k in range(SUB)]
    for distance in heads_distances():
        blocks = blocks + [(k, d ^ distance) for k, d in blocks]
    return blocks


def first_sum(make, rows):
    half = rows // 2
    distance = heads_distances()[-1]
    away = swap(make(half, rows).astype(low), "heads", distance)
    return make(0, half) + away.astype(wide)


def other_sums(x):
    for distance in reversed(heads_distances()[:-1]):
        half = x.shape[0] // 2
        x = x[:half] + swap(x[half:].astype(low), "heads", distance).astype(wide)
    return x


def sub_sum(x):
    few = x.shape[0] // SUB
    total = x[:few]
    for k, distance in enumerate(sub_distances()):
        away = swap(x[(k + 1) * few : (k + 2) * few].astype(low), "fsdp", distance)
        total = total + away.astype(wide)
    return total


def heads_in_place(x):
    devices = lax.axis_size("heads")
    me_heads = lax.axis_index("heads")
    order = [0]
    for distance in heads_distances():
        order = order + [distance ^ d for d in order]

    def place(offset):
        return sum(jnp.where(offset == d, i, 0) for i, d in enumerate(order))

    blocks = x.reshape((devices, -1) + x.shape[1:])
    return jnp.concatenate(
        [
            lax.dynamic_index_in_dim(blocks, place(me_heads ^ d), 0, keepdims=False)
            for d in range(devices)
        ],
        axis=0,
    )


def sub_exchange(x):
    devices = lax.axis_size("fsdp")
    teams = devices // SUB
    groups = [[g * teams + t for g in range(SUB)] for t in range(teams)]
    return lax.all_to_all(x, "fsdp", 0, 0, axis_index_groups=groups, tiled=True)


def teams_pieces(x):
    teams = lax.axis_size("fsdp") // SUB
    return [x] + [swap(x, "fsdp", k) for k in range(1, teams)]


def teams_halves(x):
    teams = lax.axis_size("fsdp") // SUB
    halves = (x[: SUB // 2], x[SUB // 2 :])
    return [[swap(half, "fsdp", k) for k in range(1, teams)] for half in halves]


def own_team_first(x):
    teams = lax.axis_size("fsdp") // SUB
    me_team = lax.axis_index("fsdp") % teams
    blocks = x.reshape(x.shape[0], SUB, teams, -1)
    if teams == 2:
        first, second = (blocks[:, :, t].reshape(x.shape[0], -1) for t in range(2))
        swapped = me_team == 1
        return jnp.concatenate(
            [jnp.where(swapped, second, first), jnp.where(swapped, first, second)], axis=1
        )
    blocks = jnp.take(blocks, jnp.arange(teams) ^ me_team, axis=2)
    return jnp.swapaxes(blocks, 1, 2).reshape(x.shape)


def teams_in_place(x):
    teams = lax.axis_size("fsdp") // SUB
    me_team = lax.axis_index("fsdp") % teams
    blocks = x.reshape(x.shape[0], teams, SUB, -1)
    if teams == 2:
        swapped = me_team == 1
        pair = [
            jnp.where(swapped, blocks[:, 1], blocks[:, 0]),
            jnp.where(swapped, blocks[:, 0], blocks[:, 1]),
        ]
        return jnp.stack(pair, axis=2).reshape(x.shape)
    blocks = jnp.take(blocks, jnp.arange(teams) ^ me_team, axis=1)
    return jnp.swapaxes(blocks, 1, 2).reshape(x.shape)


def teams_sum(make):
    teams = lax.axis_size("fsdp") // SUB
    away = [swap(make(k).astype(low), "fsdp", k) for k in range(1, teams)]
    total = make(0)
    for piece in away:
        total = total + piece.astype(wide)
    return total.astype(low)


def wider(x, size, axis):
    missing = [(0, 0)] * x.ndim
    missing[axis] = (0, size - x.shape[axis])
    return jnp.pad(x, missing)


def over_rows(left, right):
    return lax.dot_general(left, right, (((0,), (0,)), ((), ())), preferred_element_type=wide)


def over_cols(left, right):
    return lax.dot_general(left, right, (((1,), (1,)), ((), ())), preferred_element_type=wide)


def on_device(
    activations,
    norm_gains,
    w_query,
    w_keyval,
    w_out,
    w_gateup,
    w_down,
    seq_lengths,
    token_slot,
    out_grad,
):
    devices = lax.axis_size("fsdp")
    head_devices = lax.axis_size("heads")
    teams = devices // SUB
    me_heads = lax.axis_index("heads")
    me_team = lax.axis_index("fsdp") % teams
    me_sub = lax.axis_index("fsdp") // teams
    tok_rows, width = activations.shape
    few = tok_rows // head_devices
    rows = SUB * tok_rows
    cols = width // devices
    groups = w_query.shape[2] // HD // SUB
    query_width = groups * HD
    units = w_down.shape[0]
    sub_units = -(-units // (SUB * 128)) * 128
    qkv_width = query_width + 2 * HD
    lanes = max(qkv_width, cols)
    team_width = SUB * cols

    def share(x):
        return lax.dynamic_slice_in_dim(x, me_heads * few, few, 0)

    x_sub = sub_gather(own_team_first(share(activations)))

    extras = jnp.concatenate(
        [
            wider(norm_gains, lanes, 1),
            wider((token_slot // 128).astype(low)[None], lanes, 1),
            wider((token_slot % 128).astype(low)[None], lanes, 1),
            jnp.zeros((12, lanes), low),
        ],
        axis=0,
    )
    extras = lax.optimization_barrier(extras)
    attention_parts = jnp.stack(
        [
            jnp.concatenate(
                [
                    wider(
                        jnp.concatenate(
                            [
                                w_query[:, 0, k * query_width : (k + 1) * query_width],
                                w_keyval[:, 0],
                            ],
                            axis=1,
                        ),
                        lanes,
                        1,
                    ),
                    wider(w_out[0, k * query_width : (k + 1) * query_width], lanes, 1),
                    extras,
                ],
                axis=0,
            )
            for k in range(SUB)
        ],
        axis=0,
    )
    attention_here = sub_exchange(attention_parts)
    attention_pieces = teams_pieces(attention_here)
    out_w = jnp.concatenate(
        [
            piece[z, cols : cols + query_width, :cols]
            for piece in attention_pieces
            for z in range(SUB)
        ],
        axis=1,
    )
    x_group = heads_gather(x_sub, (attention_here,))
    qkv_w = jnp.concatenate(
        [piece[:, :cols, :qkv_width].reshape(team_width, qkv_width) for piece in attention_pieces],
        axis=0,
    )
    extras_all = jnp.stack([piece[:, cols + query_width :] for piece in attention_pieces], axis=0)
    gains = jnp.swapaxes(extras_all[:, :, :2, :cols].reshape(devices, 2, cols), 0, 1)
    gains = gains.reshape(2, width).astype(wide)
    slot_parts = extras_all[:, :, 2:4, :tok_rows].astype(jnp.int32)
    slot_blocks = (slot_parts[:, :, 0] * 128 + slot_parts[:, :, 1]).reshape(
        devices * head_devices, few
    )
    block_places = [
        ((t * SUB + (me_sub ^ k)) * head_devices) + (me_heads ^ d)
        for t in range(teams)
        for k, d in group_blocks()
    ]
    slot_all = jnp.take(slot_blocks, jnp.stack(block_places), axis=0).reshape(teams * rows)
    slot_group = slot_all[:rows]

    gateup_parts = wider(w_gateup, SUB * sub_units, 2)
    gateup_parts = jnp.stack(
        [
            jnp.concatenate(
                [gateup_parts[:, c, k * sub_units : (k + 1) * sub_units] for c in range(2)], axis=1
            )
            for k in range(SUB)
        ],
        axis=0,
    )
    gateup_here = sub_exchange(after(gateup_parts, attention_here))
    gateup_halves = teams_halves(gateup_here)
    down_parts = wider(w_down, SUB * sub_units, 0).reshape(SUB, sub_units, cols)
    down_here = sub_exchange(after(down_parts, gateup_here))
    down_pieces = teams_pieces(down_here)
    down_w = jnp.concatenate([piece[z] for piece in down_pieces for z in range(SUB)], axis=1)
    upstream_share = lax.optimization_barrier(own_team_first(share(out_grad)))
    upstream_sub = sub_gather(after(upstream_share, attention_here))
    upstream_group = heads_gather(upstream_sub)

    first_slot, position = locate(seq_lengths, slot_group)
    cosine_table, sine_table = rotation(position)
    inputs = x_group.astype(wide)
    scale_one = scale_of(inputs)
    normed_one = inputs * scale_one
    lowered_one = after((normed_one * gains[0]).astype(low), upstream_share)
    qkv_lin = jnp.dot(lowered_one, qkv_w, preferred_element_type=wide)
    queries = rotate(
        qkv_lin[:, :query_width].reshape(rows, groups, HD), cosine_table, sine_table
    ).astype(low)
    queries = after(queries, upstream_sub)
    key_rows = rotate(
        qkv_lin[:, query_width : query_width + HD], cosine_table, sine_table
    ).astype(low)
    keyvals = jnp.concatenate([key_rows, qkv_lin[:, query_width + HD :].astype(low)], axis=-1)
    key_all = jnp.concatenate(
        [keyvals] + [swap(keyvals, "fsdp", k) for k in range(1, teams)], axis=0
    )
    total_keys = key_all.shape[0]
    block_rows = divisor_rows(total_keys, 1024)
    key_blocks = (
        key_all.reshape(total_keys // block_rows, block_rows, 2 * HD),
        slot_all.reshape(total_keys // block_rows, block_rows),
    )
    slot_column = slot_group[:, None]
    first_column = first_slot[:, None]

    def scores_of(key_block, slot_block):
        logits = (
            jnp.einsum("tqd,kd->tqk", queries, key_block, preferred_element_type=wide) * 0.125
        )
        allowed = (slot_block[None, :] <= slot_column) & (slot_block[None, :] >= first_column)
        return (logits, allowed[:, None, :])

    def absorb(running, blocks):
        running_max, running_sum, running_out = running
        key_block, slot_block = blocks
        logits, allowed = scores_of(key_block[:, :HD], slot_block)
        newest = jnp.maximum(running_max, jnp.max(jnp.where(allowed, logits, masked_fill), axis=-1))
        weights = jnp.where(allowed, jnp.exp(logits - newest[..., None]), 0.0)
        factor = jnp.exp(running_max - newest)
        running_sum = running_sum * factor + jnp.sum(weights, axis=-1)
        running_out = running_out * factor[..., None] + jnp.einsum(
            "tqk,kd->tqd", weights.astype(low), key_block[:, HD:], preferred_element_type=wide
        )
        return ((newest, running_sum, running_out), None)

    start_state = (
        jnp.full((rows, groups), masked_fill, wide),
        jnp.zeros((rows, groups), wide),
        jnp.zeros((rows, groups, HD), wide),
    )
    (final_max, final_sum, final_out), unused = lax.scan(absorb, start_state, key_blocks)
    attended = final_out / final_sum[..., None]
    log_total = final_max + jnp.log(final_sum)
    attended_low = attended.reshape(rows, query_width).astype(low)
    attended_low = after(attended_low, upstream_group, gateup_here)
    branch = first_sum(
        lambda first, end: jnp.dot(attended_low[first:end], out_w, preferred_element_type=wide),
        rows,
    )
    branch = sub_sum(after(other_sums(branch), down_here, *gateup_halves[0]))

    middle = inputs[:few] + branch
    scale_two = scale_of(middle)
    normed_two = middle * scale_two
    lowered_sub = sub_gather((normed_two * gains[1]).astype(low))
    gateup_first, *gateup_others = after((gateup_here, *zip(*gateup_halves)), lowered_sub)
    gu_w = jnp.concatenate(
        [gateup_first] + [half for pair in gateup_others for half in pair], axis=0
    ).reshape(width, 2 * sub_units)
    lowered_group = heads_gather(after(lowered_sub, *gateup_halves[1]))
    hidden_grad = over_cols(upstream_group, down_w)
    gateup = jnp.dot(lowered_group, gu_w, preferred_element_type=wide)
    gate_pre = gateup[:, :sub_units]
    up_pre = gateup[:, sub_units:]
    sigmoid_gate = jax.nn.sigmoid(gate_pre)
    activated = gate_pre * sigmoid_gate
    hidden = (activated * up_pre).astype(low)
    gate_grad = hidden_grad * up_pre * sigmoid_gate * (1.0 + gate_pre * (1.0 - sigmoid_gate))
    up_grad = hidden_grad * activated
    gu_grad = jnp.concatenate([gate_grad, up_grad], axis=1).astype(low)
    half_grad_two = first_sum(lambda first, end: over_cols(gu_grad[first:end], gu_w), rows)

    def team_cols(x, k):
        return x[:, k * team_width : (k + 1) * team_width]

    late_lowered, late_hidden = (after(x, half_grad_two) for x in (lowered_group, hidden))
    half_sub = SUB // 2

    def half_cols(x, k, half):
        first = k * team_width + half * half_sub * cols
        return x[:, first : first + half_sub * cols]

    def gateup_term(half):
        return lambda k: over_rows(half_cols(late_lowered, k, half), gu_grad).reshape(
            half_sub, cols, 2 * sub_units
        )

    def down_term(k):
        term = over_rows(late_hidden, team_cols(upstream_group, k))
        return jnp.moveaxis(term.reshape(sub_units, SUB, cols), 1, 0)

    gateup_sums = [teams_sum(gateup_term(half)) for half in range(2)]
    lowered_grad_two = sub_sum(after(other_sums(half_grad_two), gateup_sums[0]))
    mixed = other_sums(
        first_sum(
            lambda first, end: jnp.dot(
                late_hidden[first:end], down_w, preferred_element_type=wide
            ),
            rows,
        )
    )
    gain_grad_two = jnp.sum(lowered_grad_two * normed_two, axis=0)
    middle_grad = upstream_share.astype(wide) + norm_back(
        scale_two, normed_two, lowered_grad_two * gains[1]
    )
    branch_sub = sub_gather(middle_grad.astype(low))
    branch_grad = heads_gather(after(branch_sub, mixed, gateup_sums[1]))
    gateup_owned = sub_exchange(after(jnp.concatenate(gateup_sums, axis=0), branch_sub))
    down_sum = teams_sum(down_term)
    down_owned = sub_exchange(after(down_sum, gateup_owned))
    mixed = sub_sum(after(mixed, branch_sub))
    block_out = teams_in_place((middle + mixed).astype(low))
    block_out = heads_in_place(heads_gather(block_out))

    attended_grad = over_cols(branch_grad, out_w).reshape(rows, groups, HD).astype(low)
    delta = jnp.sum(attended_grad.astype(wide) * attended, axis=-1)

    def backstep(query_grad, blocks):
        key_block, slot_block = blocks
        logits, allowed = scores_of(key_block[:, :HD], slot_block)
        probs = jnp.where(allowed, jnp.exp(logits - log_total[..., None]), 0.0)
        value_grad = jnp.einsum(
            "tqk,tqd->kd", probs.astype(low), attended_grad, preferred_element_type=wide
        )
        prob_grad = jnp.einsum(
            "tqd,kd->tqk", attended_grad, key_block[:, HD:], preferred_element_type=wide
        )
        score_grad = (probs * (prob_grad - delta[..., None])).astype(low)
        query_grad = query_grad + 0.125 * jnp.einsum(
            "tqk,kd->tqd", score_grad, key_block[:, :HD], preferred_element_type=wide
        )
        key_grad = 0.125 * jnp.einsum(
            "tqk,tqd->kd", score_grad, queries, preferred_element_type=wide
        )
        return (query_grad, jnp.concatenate([key_grad, value_grad], axis=-1))

    query_grad, keyval_terms = lax.scan(
        backstep, jnp.zeros((rows, groups, HD), wide), key_blocks
    )
    keyval_terms = keyval_terms.reshape(teams, rows, 2 * HD)
    keyval_sum = keyval_terms[0]
    for k in range(1, teams):
        keyval_sum = keyval_sum + swap(keyval_terms[k].astype(low), "fsdp", k).astype(wide)
    key_unrotated = rotate(keyval_sum[:, :HD], cosine_table, -sine_table)
    query_unrotated = rotate(query_grad, cosine_table, -sine_table).reshape(rows, query_width)
    qkv_grad = jnp.concatenate(
        [query_unrotated, key_unrotated, keyval_sum[:, HD:]], axis=-1
    ).astype(low)
    qkv_grad = after(qkv_grad, mixed, down_sum)
    half_grad_one = first_sum(lambda first, end: over_cols(qkv_grad[first:end], qkv_w), rows)
    lowered_grad_one = other_sums(after(half_grad_one, gateup_owned))
    def attention_term(k):
        late_grad = after(qkv_grad, half_grad_one)
        qkv_term = over_rows(team_cols(lowered_one, k), late_grad)
        gain_term = jnp.sum(
            qkv_term * qkv_w[k * team_width : (k + 1) * team_width].astype(wide), axis=1
        ).reshape(SUB, 1, cols)
        gain_two_term = gain_grad_two[k * team_width : (k + 1) * team_width].reshape(SUB, 1, cols)
        gain_terms = jnp.concatenate([gain_term, gain_two_term], axis=1)
        out_term = over_rows(attended_low, team_cols(branch_grad, k))
        out_term = jnp.moveaxis(out_term.reshape(query_width, SUB, cols), 1, 0)
        return jnp.concatenate(
            [
                wider(qkv_term.reshape(SUB, cols, qkv_width), lanes, 2),
                wider(out_term, lanes, 2),
                wider(wider(gain_terms, lanes, 2), 16, 1),
            ],
            axis=1,
        )

    attention_sum = teams_sum(attention_term)
    lowered_grad_one = sub_sum(after(lowered_grad_one, down_owned, attention_sum))
    input_grad = middle_grad + norm_back(
        scale_one[:few], normed_one[:few], lowered_grad_one * gains[0]
    )

    attention_owned = sub_exchange(attention_sum).astype(wide)
    query_owned = jnp.concatenate(
        [attention_owned[k, :cols, :query_width] for k in range(SUB)], axis=1
    )[:, None]
    keyval_owned = jnp.sum(attention_owned[:, :cols, query_width:qkv_width], axis=0)[:, None]
    out_owned = attention_owned[:, cols : cols + query_width, :cols].reshape(
        1, SUB * query_width, cols
    )
    gains_owned = jnp.sum(
        attention_owned[:, cols + query_width : cols + query_width + 2, :cols], axis=0
    )
    for distance in heads_distances():
        gains_owned = gains_owned + swap(gains_owned, "heads", distance)
    gains_owned = jnp.stack([gains_owned[0] / norm_gains[0].astype(wide), gains_owned[1]], axis=0)
    input_grad = after(teams_in_place(input_grad.astype(low)), block_out)
    input_grad = lax.all_gather(input_grad, "heads", axis=0, tiled=True).astype(wide)
    gateup_owned = jnp.stack(
        [
            jnp.concatenate(
                [gateup_owned[k, :cols, c * sub_units : (c + 1) * sub_units] for k in range(SUB)],
                axis=1,
            )[:, :units]
            for c in range(2)
        ],
        axis=1,
    ).astype(wide)
    down_owned = down_owned.reshape(SUB * sub_units, cols)[:units].astype(wide)
    return (
        block_out,
        input_grad,
        gains_owned,
        query_owned,
        keyval_owned,
        out_owned,
        gateup_owned,
        down_owned,
    )


def solution(mesh):
    placed = (
        P("fsdp", None),
        P(None, "fsdp"),
        P("fsdp", "heads", None),
        P("fsdp", "heads", None),
        P("heads", None, "fsdp"),
        P("fsdp", None, "heads"),
        P("heads", "fsdp"),
        P(),
        P("fsdp"),
        P("fsdp", None),
    )
    return jax.shard_map(
        on_device,
        mesh=mesh,
        in_specs=placed,
        out_specs=(
            P("fsdp", None),
            P("fsdp", None),
            P(None, "fsdp"),
            P("fsdp", "heads", None),
            P("fsdp", "heads", None),
            P("heads", None, "fsdp"),
            P("fsdp", None, "heads"),
            P("heads", "fsdp"),
        ),
        check_vma=False,
    )
```

```python
import jax
import jax.numpy as jnp
from jax import lax
from jax.sharding import PartitionSpec as P

HD = 64
SUB = 4


epsilon = 1e-05
rope_base = 10000.0
masked_fill = -1e30
low = jnp.bfloat16
wide = jnp.float32


def locate(seq_lengths, slot_values):
    seq_ends = jnp.cumsum(seq_lengths)
    seq_starts = seq_ends - seq_lengths
    inside = (slot_values[:, None] >= seq_starts[None, :]) & (
        slot_values[:, None] < seq_ends[None, :]
    )
    first_slot = jnp.sum(jnp.where(inside, seq_starts[None, :], 0), axis=1)
    return (first_slot, slot_values - first_slot)


def rotation(position):
    half_width = HD // 2
    frequency = rope_base ** (-jnp.arange(half_width, dtype=wide) * 2.0 / HD)
    angles = position.astype(wide)[:, None] * frequency[None, :]
    return (jnp.cos(angles), jnp.sin(angles))


def rotate(values, cosine_table, sine_table):
    half_width = values.shape[-1] // 2
    table_shape = (cosine_table.shape[0],) + (1,) * (values.ndim - 2) + (half_width,)
    cosine_part = cosine_table.reshape(table_shape)
    sine_part = sine_table.reshape(table_shape)
    first_half = values[..., :half_width]
    second_half = values[..., half_width:]
    return jnp.concatenate(
        [
            first_half * cosine_part - second_half * sine_part,
            second_half * cosine_part + first_half * sine_part,
        ],
        axis=-1,
    )


def scale_of(values):
    return lax.rsqrt(jnp.mean(values * values, axis=-1, keepdims=True) + epsilon)


def norm_back(scale, normed, incoming):
    return scale * (incoming - normed * jnp.mean(incoming * normed, axis=-1, keepdims=True))


def divisor_rows(total_rows, row_limit):
    for candidate in range(min(total_rows, row_limit), 0, -1):
        if total_rows % candidate == 0:
            return candidate
    return 1


def swap(x, axis, distance):
    size = lax.axis_size(axis)
    return lax.ppermute(x, axis, [(i, i ^ distance) for i in range(size)])


def after(x, *others):
    return lax.optimization_barrier((x,) + others)[0]


def to_all(x, axis):
    size = lax.axis_size(axis)
    copies = jnp.broadcast_to(x[None], (size,) + x.shape)
    return lax.all_to_all(copies, axis, 0, 0, tiled=True)


def heads_distances():
    distances = []
    step = lax.axis_size("heads") // 2
    while step >= 1:
        distances.append(step)
        step //= 2
    return distances


def sub_distances():
    teams = lax.axis_size("fsdp") // SUB
    return [k * teams for k in range(1, SUB)]


def sub_gather(x):
    return jnp.concatenate([x] + [swap(x, "fsdp", d) for d in sub_distances()], axis=0)


def heads_gather(x, earlier=()):
    *others, last = heads_distances()
    for distance in others:
        x = jnp.concatenate([x, swap(x, "heads", distance)], axis=0)
    if earlier:
        x = after(x, *earlier)
    return jnp.concatenate([x, swap(x, "heads", last)], axis=0)


def group_gather(x, earlier=()):
    x = sub_gather(x)
    if earlier:
        x = after(x, *earlier)
    return heads_gather(x)


def group_blocks():
    blocks = [(k, 0) for k in range(SUB)]
    for distance in heads_distances():
        blocks = blocks + [(k, d ^ distance) for k, d in blocks]
    return blocks


def first_sum(make, rows):
    half = rows // 2
    distance = heads_distances()[-1]
    away = swap(make(half, rows).astype(low), "heads", distance)
    return make(0, half) + away.astype(wide)


def other_sums(x):
    for distance in reversed(heads_distances()[:-1]):
        half = x.shape[0] // 2
        x = x[:half] + swap(x[half:].astype(low), "heads", distance).astype(wide)
    return x


def sub_sum(x):
    few = x.shape[0] // SUB
    total = x[:few]
    for k, distance in enumerate(sub_distances()):
        away = swap(x[(k + 1) * few : (k + 2) * few].astype(low), "fsdp", distance)
        total = total + away.astype(wide)
    return total


def heads_in_place(x):
    devices = lax.axis_size("heads")
    me_heads = lax.axis_index("heads")
    order = [0]
    for distance in heads_distances():
        order = order + [distance ^ d for d in order]

    def place(offset):
        return sum(jnp.where(offset == d, i, 0) for i, d in enumerate(order))

    blocks = x.reshape((devices, -1) + x.shape[1:])
    return jnp.concatenate(
        [
            lax.dynamic_index_in_dim(blocks, place(me_heads ^ d), 0, keepdims=False)
            for d in range(devices)
        ],
        axis=0,
    )


def sub_exchange(x):
    devices = lax.axis_size("fsdp")
    teams = devices // SUB
    groups = [[g * teams + t for g in range(SUB)] for t in range(teams)]
    return lax.all_to_all(x, "fsdp", 0, 0, axis_index_groups=groups, tiled=True)


def teams_pieces(x):
    teams = lax.axis_size("fsdp") // SUB
    return [x] + [swap(x, "fsdp", k) for k in range(1, teams)]


def teams_halves(x):
    teams = lax.axis_size("fsdp") // SUB
    halves = (x[: SUB // 2], x[SUB // 2 :])
    return [[swap(half, "fsdp", k) for k in range(1, teams)] for half in halves]


def own_team_first(x):
    teams = lax.axis_size("fsdp") // SUB
    me_team = lax.axis_index("fsdp") % teams
    blocks = x.reshape(x.shape[0], SUB, teams, -1)
    if teams == 2:
        first, second = (blocks[:, :, t].reshape(x.shape[0], -1) for t in range(2))
        swapped = me_team == 1
        return jnp.concatenate(
            [jnp.where(swapped, second, first), jnp.where(swapped, first, second)], axis=1
        )
    blocks = jnp.take(blocks, jnp.arange(teams) ^ me_team, axis=2)
    return jnp.swapaxes(blocks, 1, 2).reshape(x.shape)


def teams_in_place(x):
    teams = lax.axis_size("fsdp") // SUB
    me_team = lax.axis_index("fsdp") % teams
    blocks = x.reshape(x.shape[0], teams, SUB, -1)
    if teams == 2:
        swapped = me_team == 1
        pair = [
            jnp.where(swapped, blocks[:, 1], blocks[:, 0]),
            jnp.where(swapped, blocks[:, 0], blocks[:, 1]),
        ]
        return jnp.stack(pair, axis=2).reshape(x.shape)
    blocks = jnp.take(blocks, jnp.arange(teams) ^ me_team, axis=1)
    return jnp.swapaxes(blocks, 1, 2).reshape(x.shape)


def teams_sum(make):
    teams = lax.axis_size("fsdp") // SUB
    away = [swap(make(k).astype(low), "fsdp", k) for k in range(1, teams)]
    total = make(0)
    for piece in away:
        total = total + piece.astype(wide)
    return total.astype(low)


def wider(x, size, axis):
    missing = [(0, 0)] * x.ndim
    missing[axis] = (0, size - x.shape[axis])
    return jnp.pad(x, missing)


def over_rows(left, right):
    return lax.dot_general(left, right, (((0,), (0,)), ((), ())), preferred_element_type=wide)


def over_cols(left, right):
    return lax.dot_general(left, right, (((1,), (1,)), ((), ())), preferred_element_type=wide)


def on_device(
    activations,
    norm_gains,
    w_query,
    w_keyval,
    w_out,
    w_gateup,
    w_down,
    seq_lengths,
    token_slot,
    out_grad,
):
    devices = lax.axis_size("fsdp")
    head_devices = lax.axis_size("heads")
    teams = devices // SUB
    me_heads = lax.axis_index("heads")
    me_team = lax.axis_index("fsdp") % teams
    me_sub = lax.axis_index("fsdp") // teams
    tok_rows, width = activations.shape
    few = tok_rows // head_devices
    rows = SUB * tok_rows
    cols = width // devices
    groups = w_query.shape[2] // HD // SUB
    query_width = groups * HD
    units = w_down.shape[0]
    sub_units = -(-units // (SUB * 128)) * 128
    qkv_width = query_width + 2 * HD
    lanes = max(qkv_width, cols)
    team_width = SUB * cols

    def share(x):
        return lax.dynamic_slice_in_dim(x, me_heads * few, few, 0)

    x_sub = sub_gather(own_team_first(share(activations)))

    extras = jnp.concatenate(
        [
            wider(norm_gains, lanes, 1),
            wider((token_slot // 128).astype(low)[None], lanes, 1),
            wider((token_slot % 128).astype(low)[None], lanes, 1),
            jnp.zeros((12, lanes), low),
        ],
        axis=0,
    )
    extras = lax.optimization_barrier(extras)
    attention_parts = jnp.stack(
        [
            jnp.concatenate(
                [
                    wider(
                        jnp.concatenate(
                            [
                                w_query[:, 0, k * query_width : (k + 1) * query_width],
                                w_keyval[:, 0],
                            ],
                            axis=1,
                        ),
                        lanes,
                        1,
                    ),
                    wider(w_out[0, k * query_width : (k + 1) * query_width], lanes, 1),
                    extras,
                ],
                axis=0,
            )
            for k in range(SUB)
        ],
        axis=0,
    )
    attention_here = sub_exchange(attention_parts)
    attention_pieces = teams_pieces(attention_here)
    x_group = heads_gather(x_sub, (attention_here,))
    qkv_w = jnp.concatenate(
        [piece[:, :cols, :qkv_width].reshape(team_width, qkv_width) for piece in attention_pieces],
        axis=0,
    )
    extras_all = jnp.stack([piece[:, cols + query_width :] for piece in attention_pieces], axis=0)
    gains = jnp.swapaxes(extras_all[:, :, :2, :cols].reshape(devices, 2, cols), 0, 1)
    gains = gains.reshape(2, width).astype(wide)
    slot_parts = extras_all[:, :, 2:4, :tok_rows].astype(jnp.int32)
    slot_blocks = (slot_parts[:, :, 0] * 128 + slot_parts[:, :, 1]).reshape(
        devices * head_devices, few
    )
    block_places = [
        ((t * SUB + (me_sub ^ k)) * head_devices) + (me_heads ^ d)
        for t in range(teams)
        for k, d in group_blocks()
    ]
    slot_all = jnp.take(slot_blocks, jnp.stack(block_places), axis=0).reshape(teams * rows)
    slot_group = slot_all[:rows]

    gateup_parts = wider(w_gateup, SUB * sub_units, 2)
    gateup_parts = jnp.stack(
        [
            jnp.concatenate(
                [gateup_parts[:, c, k * sub_units : (k + 1) * sub_units] for c in range(2)], axis=1
            )
            for k in range(SUB)
        ],
        axis=0,
    )
    gateup_here = sub_exchange(after(gateup_parts, attention_here))
    gateup_halves = teams_halves(gateup_here)
    down_parts = wider(w_down, SUB * sub_units, 0).reshape(SUB, sub_units, cols)
    down_here = sub_exchange(after(down_parts, gateup_here))
    down_pieces = teams_pieces(down_here)
    down_w = jnp.concatenate([piece[z] for piece in down_pieces for z in range(SUB)], axis=1)
    upstream_share = lax.optimization_barrier(own_team_first(share(out_grad)))
    upstream_sub = sub_gather(after(upstream_share, attention_here))
    upstream_group = heads_gather(upstream_sub)

    first_slot, position = locate(seq_lengths, slot_group)
    cosine_table, sine_table = rotation(position)
    inputs = x_group.astype(wide)
    scale_one = scale_of(inputs)
    normed_one = inputs * scale_one
    lowered_one = after((normed_one * gains[0]).astype(low), upstream_share)
    qkv_lin = jnp.dot(lowered_one, qkv_w, preferred_element_type=wide)
    queries = rotate(
        qkv_lin[:, :query_width].reshape(rows, groups, HD), cosine_table, sine_table
    ).astype(low)
    queries = after(queries, upstream_sub)
    out_w = jnp.concatenate(
        [
            after(piece[:, cols : cols + query_width, :cols], queries)[z]
            for piece in attention_pieces
            for z in range(SUB)
        ],
        axis=1,
    )
    key_rows = rotate(
        qkv_lin[:, query_width : query_width + HD], cosine_table, sine_table
    ).astype(low)
    keyvals = jnp.concatenate([key_rows, qkv_lin[:, query_width + HD :].astype(low)], axis=-1)
    key_all = jnp.concatenate(
        [keyvals] + [swap(keyvals, "fsdp", k) for k in range(1, teams)], axis=0
    )
    total_keys = key_all.shape[0]
    block_rows = divisor_rows(total_keys, 1024)
    key_blocks = (
        key_all.reshape(total_keys // block_rows, block_rows, 2 * HD),
        slot_all.reshape(total_keys // block_rows, block_rows),
    )
    slot_column = slot_group[:, None]
    first_column = first_slot[:, None]

    def scores_of(key_block, slot_block):
        logits = (
            jnp.einsum("tqd,kd->tqk", queries, key_block, preferred_element_type=wide) * 0.125
        )
        allowed = (slot_block[None, :] <= slot_column) & (slot_block[None, :] >= first_column)
        return (logits, allowed[:, None, :])

    def absorb(running, blocks):
        running_max, running_sum, running_out = running
        key_block, slot_block = blocks
        logits, allowed = scores_of(key_block[:, :HD], slot_block)
        newest = jnp.maximum(running_max, jnp.max(jnp.where(allowed, logits, masked_fill), axis=-1))
        weights = jnp.where(allowed, jnp.exp(logits - newest[..., None]), 0.0)
        factor = jnp.exp(running_max - newest)
        running_sum = running_sum * factor + jnp.sum(weights, axis=-1)
        running_out = running_out * factor[..., None] + jnp.einsum(
            "tqk,kd->tqd", weights.astype(low), key_block[:, HD:], preferred_element_type=wide
        )
        return ((newest, running_sum, running_out), None)

    start_state = (
        jnp.full((rows, groups), masked_fill, wide),
        jnp.zeros((rows, groups), wide),
        jnp.zeros((rows, groups, HD), wide),
    )
    (final_max, final_sum, final_out), unused = lax.scan(absorb, start_state, key_blocks)
    attended = final_out / final_sum[..., None]
    log_total = final_max + jnp.log(final_sum)
    attended_low = attended.reshape(rows, query_width).astype(low)
    attended_low = after(attended_low, upstream_group, gateup_here)
    branch = first_sum(
        lambda first, end: jnp.dot(attended_low[first:end], out_w, preferred_element_type=wide),
        rows,
    )
    branch = sub_sum(after(other_sums(branch), down_here, *gateup_halves[0]))

    middle = inputs[:few] + branch
    scale_two = scale_of(middle)
    normed_two = middle * scale_two
    lowered_sub = sub_gather((normed_two * gains[1]).astype(low))
    gateup_first, *gateup_others = after((gateup_here, *zip(*gateup_halves)), lowered_sub)
    gu_w = jnp.concatenate(
        [gateup_first] + [half for pair in gateup_others for half in pair], axis=0
    ).reshape(width, 2 * sub_units)
    lowered_group = heads_gather(after(lowered_sub, *gateup_halves[1]))
    hidden_grad = over_cols(upstream_group, down_w)
    gateup = jnp.dot(lowered_group, gu_w, preferred_element_type=wide)
    gate_pre = gateup[:, :sub_units]
    up_pre = gateup[:, sub_units:]
    sigmoid_gate = jax.nn.sigmoid(gate_pre)
    activated = gate_pre * sigmoid_gate
    hidden = (activated * up_pre).astype(low)
    gate_grad = hidden_grad * up_pre * sigmoid_gate * (1.0 + gate_pre * (1.0 - sigmoid_gate))
    up_grad = hidden_grad * activated
    gu_grad = jnp.concatenate([gate_grad, up_grad], axis=1).astype(low)
    half_grad_two = first_sum(lambda first, end: over_cols(gu_grad[first:end], gu_w), rows)

    def team_cols(x, k):
        return x[:, k * team_width : (k + 1) * team_width]

    late_lowered, late_hidden = (after(x, half_grad_two) for x in (lowered_group, hidden))
    half_sub = SUB // 2

    def half_cols(x, k, half):
        first = k * team_width + half * half_sub * cols
        return x[:, first : first + half_sub * cols]

    def gateup_term(half):
        return lambda k: over_rows(half_cols(late_lowered, k, half), gu_grad).reshape(
            half_sub, cols, 2 * sub_units
        )

    def down_term(k):
        term = over_rows(late_hidden, team_cols(upstream_group, k))
        return jnp.moveaxis(term.reshape(sub_units, SUB, cols), 1, 0)

    gateup_sums = [teams_sum(gateup_term(half)) for half in range(2)]
    lowered_grad_two = sub_sum(other_sums(half_grad_two))
    mixed = other_sums(
        first_sum(
            lambda first, end: jnp.dot(
                late_hidden[first:end], down_w, preferred_element_type=wide
            ),
            rows,
        )
    )
    gain_grad_two = jnp.sum(lowered_grad_two * normed_two, axis=0)
    middle_grad = upstream_share.astype(wide) + norm_back(
        scale_two, normed_two, lowered_grad_two * gains[1]
    )
    branch_sub = sub_gather(after(middle_grad.astype(low), gateup_sums[0]))
    branch_grad = heads_gather(after(branch_sub, mixed, gateup_sums[1]))
    gateup_owned = sub_exchange(after(jnp.concatenate(gateup_sums, axis=0), branch_sub))
    down_sum = teams_sum(down_term)
    down_owned = sub_exchange(after(down_sum, gateup_owned))
    mixed = sub_sum(after(mixed, branch_sub))
    block_out = teams_in_place((middle + mixed).astype(low))
    block_out = heads_in_place(heads_gather(block_out))

    attended_grad = over_cols(branch_grad, out_w).reshape(rows, groups, HD).astype(low)
    delta = jnp.sum(attended_grad.astype(wide) * attended, axis=-1)

    def backstep(query_grad, blocks):
        key_block, slot_block = blocks
        logits, allowed = scores_of(key_block[:, :HD], slot_block)
        probs = jnp.where(allowed, jnp.exp(logits - log_total[..., None]), 0.0)
        value_grad = jnp.einsum(
            "tqk,tqd->kd", probs.astype(low), attended_grad, preferred_element_type=wide
        )
        prob_grad = jnp.einsum(
            "tqd,kd->tqk", attended_grad, key_block[:, HD:], preferred_element_type=wide
        )
        score_grad = (probs * (prob_grad - delta[..., None])).astype(low)
        query_grad = query_grad + 0.125 * jnp.einsum(
            "tqk,kd->tqd", score_grad, key_block[:, :HD], preferred_element_type=wide
        )
        key_grad = 0.125 * jnp.einsum(
            "tqk,tqd->kd", score_grad, queries, preferred_element_type=wide
        )
        return (query_grad, jnp.concatenate([key_grad, value_grad], axis=-1))

    query_grad, keyval_terms = lax.scan(
        backstep, jnp.zeros((rows, groups, HD), wide), key_blocks
    )
    keyval_terms = keyval_terms.reshape(teams, rows, 2 * HD)
    keyval_sum = keyval_terms[0]
    for k in range(1, teams):
        keyval_sum = keyval_sum + swap(keyval_terms[k].astype(low), "fsdp", k).astype(wide)
    key_unrotated = rotate(keyval_sum[:, :HD], cosine_table, -sine_table)
    query_unrotated = rotate(query_grad, cosine_table, -sine_table).reshape(rows, query_width)
    qkv_grad = jnp.concatenate(
        [query_unrotated, key_unrotated, keyval_sum[:, HD:]], axis=-1
    ).astype(low)
    qkv_grad = after(qkv_grad, mixed, down_sum)
    half_grad_one = first_sum(lambda first, end: over_cols(qkv_grad[first:end], qkv_w), rows)
    lowered_grad_one = other_sums(after(half_grad_one, gateup_owned))
    def attention_term(k):
        late_grad = after(qkv_grad, half_grad_one)
        qkv_term = over_rows(team_cols(lowered_one, k), late_grad)
        gain_term = jnp.sum(
            qkv_term * qkv_w[k * team_width : (k + 1) * team_width].astype(wide), axis=1
        ).reshape(SUB, 1, cols)
        gain_two_term = gain_grad_two[k * team_width : (k + 1) * team_width].reshape(SUB, 1, cols)
        gain_terms = jnp.concatenate([gain_term, gain_two_term], axis=1)
        out_term = over_rows(attended_low, team_cols(branch_grad, k))
        out_term = jnp.moveaxis(out_term.reshape(query_width, SUB, cols), 1, 0)
        return jnp.concatenate(
            [
                wider(qkv_term.reshape(SUB, cols, qkv_width), lanes, 2),
                wider(out_term, lanes, 2),
                wider(wider(gain_terms, lanes, 2), 16, 1),
            ],
            axis=1,
        )

    attention_sum = teams_sum(attention_term)
    lowered_grad_one = sub_sum(after(lowered_grad_one, down_owned))
    input_grad = middle_grad + norm_back(
        scale_one[:few], normed_one[:few], lowered_grad_one * gains[0]
    )

    attention_owned = sub_exchange(attention_sum).astype(wide)
    query_owned = jnp.concatenate(
        [attention_owned[k, :cols, :query_width] for k in range(SUB)], axis=1
    )[:, None]
    keyval_owned = jnp.sum(attention_owned[:, :cols, query_width:qkv_width], axis=0)[:, None]
    out_owned = attention_owned[:, cols : cols + query_width, :cols].reshape(
        1, SUB * query_width, cols
    )
    gains_owned = jnp.sum(
        attention_owned[:, cols + query_width : cols + query_width + 2, :cols], axis=0
    )
    gains_owned = gains_owned + sum(
        swap(gains_owned, "heads", distance) for distance in range(1, head_devices)
    )
    gains_owned = jnp.stack([gains_owned[0] / norm_gains[0].astype(wide), gains_owned[1]], axis=0)
    input_grad = after(teams_in_place(input_grad.astype(low)), block_out)
    input_grad = lax.all_gather(input_grad, "heads", axis=0, tiled=True).astype(wide)
    gateup_owned = jnp.stack(
        [
            jnp.concatenate(
                [gateup_owned[k, :cols, c * sub_units : (c + 1) * sub_units] for k in range(SUB)],
                axis=1,
            )[:, :units]
            for c in range(2)
        ],
        axis=1,
    ).astype(wide)
    down_owned = down_owned.reshape(SUB * sub_units, cols)[:units].astype(wide)
    return (
        block_out,
        input_grad,
        gains_owned,
        query_owned,
        keyval_owned,
        out_owned,
        gateup_owned,
        down_owned,
    )


def solution(mesh):
    placed = (
        P("fsdp", None),
        P(None, "fsdp"),
        P("fsdp", "heads", None),
        P("fsdp", "heads", None),
        P("heads", None, "fsdp"),
        P("fsdp", None, "heads"),
        P("heads", "fsdp"),
        P(),
        P("fsdp"),
        P("fsdp", None),
    )
    return jax.shard_map(
        on_device,
        mesh=mesh,
        in_specs=placed,
        out_specs=(
            P("fsdp", None),
            P("fsdp", None),
            P(None, "fsdp"),
            P("fsdp", "heads", None),
            P("fsdp", "heads", None),
            P("heads", None, "fsdp"),
            P("fsdp", None, "heads"),
            P("heads", "fsdp"),
        ),
        check_vma=False,
    )
```

```python
import jax
import jax.numpy as jnp
from jax import lax
from jax.sharding import PartitionSpec as P

HD = 64
SUB = 4


epsilon = 1e-05
rope_base = 10000.0
masked_fill = -1e30
low = jnp.bfloat16
wide = jnp.float32


def locate(seq_lengths, slot_values):
    seq_ends = jnp.cumsum(seq_lengths)
    seq_starts = seq_ends - seq_lengths
    inside = (slot_values[:, None] >= seq_starts[None, :]) & (
        slot_values[:, None] < seq_ends[None, :]
    )
    first_slot = jnp.sum(jnp.where(inside, seq_starts[None, :], 0), axis=1)
    return (first_slot, slot_values - first_slot)


def rotation(position):
    half_width = HD // 2
    frequency = rope_base ** (-jnp.arange(half_width, dtype=wide) * 2.0 / HD)
    angles = position.astype(wide)[:, None] * frequency[None, :]
    return (jnp.cos(angles), jnp.sin(angles))


def rotate(values, cosine_table, sine_table):
    half_width = values.shape[-1] // 2
    table_shape = (cosine_table.shape[0],) + (1,) * (values.ndim - 2) + (half_width,)
    cosine_part = cosine_table.reshape(table_shape)
    sine_part = sine_table.reshape(table_shape)
    first_half = values[..., :half_width]
    second_half = values[..., half_width:]
    return jnp.concatenate(
        [
            first_half * cosine_part - second_half * sine_part,
            second_half * cosine_part + first_half * sine_part,
        ],
        axis=-1,
    )


def scale_of(values):
    return lax.rsqrt(jnp.mean(values * values, axis=-1, keepdims=True) + epsilon)


def norm_back(scale, normed, incoming):
    return scale * (incoming - normed * jnp.mean(incoming * normed, axis=-1, keepdims=True))


def divisor_rows(total_rows, row_limit):
    for candidate in range(min(total_rows, row_limit), 0, -1):
        if total_rows % candidate == 0:
            return candidate
    return 1


def swap(x, axis, distance):
    size = lax.axis_size(axis)
    return lax.ppermute(x, axis, [(i, i ^ distance) for i in range(size)])


def after(x, *others):
    return lax.optimization_barrier((x,) + others)[0]


def to_all(x, axis):
    size = lax.axis_size(axis)
    copies = jnp.broadcast_to(x[None], (size,) + x.shape)
    return lax.all_to_all(copies, axis, 0, 0, tiled=True)


def heads_distances():
    distances = []
    step = lax.axis_size("heads") // 2
    while step >= 1:
        distances.append(step)
        step //= 2
    return distances


def sub_distances():
    teams = lax.axis_size("fsdp") // SUB
    return [k * teams for k in range(1, SUB)]


def sub_gather(x):
    return jnp.concatenate([x] + [swap(x, "fsdp", d) for d in sub_distances()], axis=0)


def heads_gather(x, earlier=()):
    *others, last = heads_distances()
    for distance in others:
        x = jnp.concatenate([x, swap(x, "heads", distance)], axis=0)
    if earlier:
        x = after(x, *earlier)
    return jnp.concatenate([x, swap(x, "heads", last)], axis=0)


def group_gather(x, earlier=()):
    x = sub_gather(x)
    if earlier:
        x = after(x, *earlier)
    return heads_gather(x)


def group_blocks():
    blocks = [(k, 0) for k in range(SUB)]
    for distance in heads_distances():
        blocks = blocks + [(k, d ^ distance) for k, d in blocks]
    return blocks


def first_sum(make, rows):
    half = rows // 2
    distance = heads_distances()[-1]
    away = swap(make(half, rows).astype(low), "heads", distance)
    return make(0, half) + away.astype(wide)


def other_sums(x):
    for distance in reversed(heads_distances()[:-1]):
        half = x.shape[0] // 2
        x = x[:half] + swap(x[half:].astype(low), "heads", distance).astype(wide)
    return x


def sub_sum(x):
    few = x.shape[0] // SUB
    total = x[:few]
    for k, distance in enumerate(sub_distances()):
        away = swap(x[(k + 1) * few : (k + 2) * few].astype(low), "fsdp", distance)
        total = total + away.astype(wide)
    return total


def heads_in_place(x):
    devices = lax.axis_size("heads")
    me_heads = lax.axis_index("heads")
    order = [0]
    for distance in heads_distances():
        order = order + [distance ^ d for d in order]

    def place(offset):
        return sum(jnp.where(offset == d, i, 0) for i, d in enumerate(order))

    blocks = x.reshape((devices, -1) + x.shape[1:])
    return jnp.concatenate(
        [
            lax.dynamic_index_in_dim(blocks, place(me_heads ^ d), 0, keepdims=False)
            for d in range(devices)
        ],
        axis=0,
    )


def sub_exchange(x):
    devices = lax.axis_size("fsdp")
    teams = devices // SUB
    groups = [[g * teams + t for g in range(SUB)] for t in range(teams)]
    return lax.all_to_all(x, "fsdp", 0, 0, axis_index_groups=groups, tiled=True)


def teams_pieces(x):
    teams = lax.axis_size("fsdp") // SUB
    return [x] + [swap(x, "fsdp", k) for k in range(1, teams)]


def teams_halves(x):
    teams = lax.axis_size("fsdp") // SUB
    halves = (x[: SUB // 2], x[SUB // 2 :])
    return [[swap(half, "fsdp", k) for k in range(1, teams)] for half in halves]


def own_team_first(x):
    teams = lax.axis_size("fsdp") // SUB
    me_team = lax.axis_index("fsdp") % teams
    blocks = x.reshape(x.shape[0], SUB, teams, -1)
    if teams == 2:
        first, second = (blocks[:, :, t].reshape(x.shape[0], -1) for t in range(2))
        swapped = me_team == 1
        return jnp.concatenate(
            [jnp.where(swapped, second, first), jnp.where(swapped, first, second)], axis=1
        )
    blocks = jnp.take(blocks, jnp.arange(teams) ^ me_team, axis=2)
    return jnp.swapaxes(blocks, 1, 2).reshape(x.shape)


def teams_in_place(x):
    teams = lax.axis_size("fsdp") // SUB
    me_team = lax.axis_index("fsdp") % teams
    blocks = x.reshape(x.shape[0], teams, SUB, -1)
    if teams == 2:
        swapped = me_team == 1
        pair = [
            jnp.where(swapped, blocks[:, 1], blocks[:, 0]),
            jnp.where(swapped, blocks[:, 0], blocks[:, 1]),
        ]
        return jnp.stack(pair, axis=2).reshape(x.shape)
    blocks = jnp.take(blocks, jnp.arange(teams) ^ me_team, axis=1)
    return jnp.swapaxes(blocks, 1, 2).reshape(x.shape)


def teams_sum(make):
    teams = lax.axis_size("fsdp") // SUB
    away = [swap(make(k).astype(low), "fsdp", k) for k in range(1, teams)]
    total = make(0)
    for piece in away:
        total = total + piece.astype(wide)
    return total.astype(low)


def wider(x, size, axis):
    missing = [(0, 0)] * x.ndim
    missing[axis] = (0, size - x.shape[axis])
    return jnp.pad(x, missing)


def over_rows(left, right):
    return lax.dot_general(left, right, (((0,), (0,)), ((), ())), preferred_element_type=wide)


def over_cols(left, right):
    return lax.dot_general(left, right, (((1,), (1,)), ((), ())), preferred_element_type=wide)


def on_device(
    activations,
    norm_gains,
    w_query,
    w_keyval,
    w_out,
    w_gateup,
    w_down,
    seq_lengths,
    token_slot,
    out_grad,
):
    devices = lax.axis_size("fsdp")
    head_devices = lax.axis_size("heads")
    teams = devices // SUB
    me_heads = lax.axis_index("heads")
    me_team = lax.axis_index("fsdp") % teams
    me_sub = lax.axis_index("fsdp") // teams
    tok_rows, width = activations.shape
    few = tok_rows // head_devices
    rows = SUB * tok_rows
    cols = width // devices
    groups = w_query.shape[2] // HD // SUB
    query_width = groups * HD
    units = w_down.shape[0]
    sub_units = -(-units // (SUB * 128)) * 128
    qkv_width = query_width + 2 * HD
    lanes = max(qkv_width, cols)
    team_width = SUB * cols

    def share(x):
        return lax.dynamic_slice_in_dim(x, me_heads * few, few, 0)

    x_sub = sub_gather(own_team_first(share(activations)))

    extras = jnp.concatenate(
        [
            wider(norm_gains, lanes, 1),
            wider((token_slot // 128).astype(low)[None], lanes, 1),
            wider((token_slot % 128).astype(low)[None], lanes, 1),
            jnp.zeros((12, lanes), low),
        ],
        axis=0,
    )
    extras = lax.optimization_barrier(extras)
    attention_parts = jnp.stack(
        [
            jnp.concatenate(
                [
                    wider(
                        jnp.concatenate(
                            [
                                w_query[:, 0, k * query_width : (k + 1) * query_width],
                                w_keyval[:, 0],
                            ],
                            axis=1,
                        ),
                        lanes,
                        1,
                    ),
                    wider(w_out[0, k * query_width : (k + 1) * query_width], lanes, 1),
                    extras,
                ],
                axis=0,
            )
            for k in range(SUB)
        ],
        axis=0,
    )
    attention_here = sub_exchange(attention_parts)
    attention_pieces = teams_pieces(attention_here)
    x_group = heads_gather(x_sub, (attention_here,))
    qkv_w = jnp.concatenate(
        [piece[:, :cols, :qkv_width].reshape(team_width, qkv_width) for piece in attention_pieces],
        axis=0,
    )
    extras_all = jnp.stack([piece[:, cols + query_width :] for piece in attention_pieces], axis=0)
    gains = jnp.swapaxes(extras_all[:, :, :2, :cols].reshape(devices, 2, cols), 0, 1)
    gains = gains.reshape(2, width).astype(wide)
    slot_parts = extras_all[:, :, 2:4, :tok_rows].astype(jnp.int32)
    slot_blocks = (slot_parts[:, :, 0] * 128 + slot_parts[:, :, 1]).reshape(
        devices * head_devices, few
    )
    block_places = [
        ((t * SUB + (me_sub ^ k)) * head_devices) + (me_heads ^ d)
        for t in range(teams)
        for k, d in group_blocks()
    ]
    slot_all = jnp.take(slot_blocks, jnp.stack(block_places), axis=0).reshape(teams * rows)
    slot_group = slot_all[:rows]

    gateup_parts = wider(w_gateup, SUB * sub_units, 2)
    gateup_parts = jnp.stack(
        [
            jnp.concatenate(
                [gateup_parts[:, c, k * sub_units : (k + 1) * sub_units] for c in range(2)], axis=1
            )
            for k in range(SUB)
        ],
        axis=0,
    )
    gateup_here = sub_exchange(after(gateup_parts, attention_here))
    gateup_halves = teams_halves(gateup_here)
    down_parts = wider(w_down, SUB * sub_units, 0).reshape(SUB, sub_units, cols)
    down_here = sub_exchange(after(down_parts, gateup_here))
    down_pieces = teams_pieces(down_here)
    down_w = jnp.concatenate([piece[z] for piece in down_pieces for z in range(SUB)], axis=1)
    upstream_share = lax.optimization_barrier(own_team_first(share(out_grad)))
    upstream_sub = sub_gather(after(upstream_share, attention_here))
    upstream_group = heads_gather(upstream_sub)

    first_slot, position = locate(seq_lengths, slot_group)
    cosine_table, sine_table = rotation(position)
    inputs = x_group.astype(wide)
    scale_one = scale_of(inputs)
    normed_one = inputs * scale_one
    lowered_one = after((normed_one * gains[0]).astype(low), upstream_share)
    qkv_lin = jnp.dot(lowered_one, qkv_w, preferred_element_type=wide)
    queries = rotate(
        qkv_lin[:, :query_width].reshape(rows, groups, HD), cosine_table, sine_table
    ).astype(low)
    queries = after(queries, upstream_sub)
    out_w = jnp.concatenate(
        [
            after(piece[:, cols : cols + query_width, :cols], queries)[z]
            for piece in attention_pieces
            for z in range(SUB)
        ],
        axis=1,
    )
    key_rows = rotate(
        qkv_lin[:, query_width : query_width + HD], cosine_table, sine_table
    ).astype(low)
    keyvals = jnp.concatenate([key_rows, qkv_lin[:, query_width + HD :].astype(low)], axis=-1)
    key_all = jnp.concatenate(
        [keyvals] + [swap(keyvals, "fsdp", k) for k in range(1, teams)], axis=0
    )
    total_keys = key_all.shape[0]
    block_rows = divisor_rows(total_keys, 1024)
    key_blocks = (
        key_all.reshape(total_keys // block_rows, block_rows, 2 * HD),
        slot_all.reshape(total_keys // block_rows, block_rows),
    )
    slot_column = slot_group[:, None]
    first_column = first_slot[:, None]

    def scores_of(key_block, slot_block):
        logits = (
            jnp.einsum("tqd,kd->tqk", queries, key_block, preferred_element_type=wide) * 0.125
        )
        allowed = (slot_block[None, :] <= slot_column) & (slot_block[None, :] >= first_column)
        return (logits, allowed[:, None, :])

    def absorb(running, blocks):
        running_max, running_sum, running_out = running
        key_block, slot_block = blocks
        logits, allowed = scores_of(key_block[:, :HD], slot_block)
        newest = jnp.maximum(running_max, jnp.max(jnp.where(allowed, logits, masked_fill), axis=-1))
        weights = jnp.where(allowed, jnp.exp(logits - newest[..., None]), 0.0)
        factor = jnp.exp(running_max - newest)
        running_sum = running_sum * factor + jnp.sum(weights, axis=-1)
        running_out = running_out * factor[..., None] + jnp.einsum(
            "tqk,kd->tqd", weights.astype(low), key_block[:, HD:], preferred_element_type=wide
        )
        return ((newest, running_sum, running_out), None)

    start_state = (
        jnp.full((rows, groups), masked_fill, wide),
        jnp.zeros((rows, groups), wide),
        jnp.zeros((rows, groups, HD), wide),
    )
    (final_max, final_sum, final_out), unused = lax.scan(absorb, start_state, key_blocks)
    attended = final_out / final_sum[..., None]
    log_total = final_max + jnp.log(final_sum)
    attended_low = attended.reshape(rows, query_width).astype(low)
    attended_low = after(attended_low, upstream_group, gateup_here)
    branch = first_sum(
        lambda first, end: jnp.dot(attended_low[first:end], out_w, preferred_element_type=wide),
        rows,
    )
    branch = sub_sum(after(other_sums(branch), down_here, *gateup_halves[0]))

    own_inputs = lax.optimization_barrier(x_group[:few]).astype(wide)
    own_scale = scale_of(own_inputs)
    own_normed = own_inputs * own_scale
    middle = own_inputs + branch
    scale_two = scale_of(middle)
    normed_two = middle * scale_two
    lowered_sub = sub_gather((normed_two * gains[1]).astype(low))
    gateup_first, *gateup_others = after((gateup_here, *zip(*gateup_halves)), lowered_sub)
    gu_w = jnp.concatenate(
        [gateup_first] + [half for pair in gateup_others for half in pair], axis=0
    ).reshape(width, 2 * sub_units)
    lowered_group = heads_gather(after(lowered_sub, *gateup_halves[1]))
    hidden_grad = over_cols(upstream_group, down_w)
    gateup = jnp.dot(lowered_group, gu_w, preferred_element_type=wide)
    gate_pre = gateup[:, :sub_units]
    up_pre = gateup[:, sub_units:]
    sigmoid_gate = jax.nn.sigmoid(gate_pre)
    activated = gate_pre * sigmoid_gate
    hidden = (activated * up_pre).astype(low)
    gate_grad = hidden_grad * up_pre * sigmoid_gate * (1.0 + gate_pre * (1.0 - sigmoid_gate))
    up_grad = hidden_grad * activated
    gu_grad = jnp.concatenate([gate_grad, up_grad], axis=1).astype(low)
    half_grad_two = first_sum(lambda first, end: over_cols(gu_grad[first:end], gu_w), rows)

    def team_cols(x, k):
        return x[:, k * team_width : (k + 1) * team_width]

    late_lowered, late_hidden = (after(x, half_grad_two) for x in (lowered_group, hidden))
    half_sub = SUB // 2

    def half_cols(x, k, half):
        first = k * team_width + half * half_sub * cols
        return x[:, first : first + half_sub * cols]

    def gateup_term(half):
        return lambda k: over_rows(half_cols(late_lowered, k, half), gu_grad).reshape(
            half_sub, cols, 2 * sub_units
        )

    def down_term(k):
        term = over_rows(late_hidden, team_cols(upstream_group, k))
        return jnp.moveaxis(term.reshape(sub_units, SUB, cols), 1, 0)

    gateup_sums = [teams_sum(gateup_term(half)) for half in range(2)]
    lowered_grad_two = sub_sum(other_sums(half_grad_two))
    mixed = other_sums(
        first_sum(
            lambda first, end: jnp.dot(
                late_hidden[first:end], down_w, preferred_element_type=wide
            ),
            rows,
        )
    )
    gain_grad_two = jnp.sum(lowered_grad_two * normed_two, axis=0)
    middle_grad = upstream_share.astype(wide) + norm_back(
        scale_two, normed_two, lowered_grad_two * gains[1]
    )
    branch_sub = sub_gather(after(middle_grad.astype(low), gateup_sums[0]))
    branch_grad = heads_gather(after(branch_sub, mixed, gateup_sums[1]))
    gateup_owned = sub_exchange(after(jnp.concatenate(gateup_sums, axis=0), branch_sub))
    down_sum = teams_sum(down_term)
    down_owned = sub_exchange(after(down_sum, gateup_owned))
    mixed = sub_sum(after(mixed, branch_sub))
    block_out = teams_in_place((middle + mixed).astype(low))
    block_out = heads_in_place(heads_gather(block_out))

    attended_grad = over_cols(branch_grad, out_w).reshape(rows, groups, HD).astype(low)
    delta = jnp.sum(attended_grad.astype(wide) * attended, axis=-1)

    def backstep(query_grad, blocks):
        key_block, slot_block = blocks
        logits, allowed = scores_of(key_block[:, :HD], slot_block)
        probs = jnp.where(allowed, jnp.exp(logits - log_total[..., None]), 0.0)
        value_grad = jnp.einsum(
            "tqk,tqd->kd", probs.astype(low), attended_grad, preferred_element_type=wide
        )
        prob_grad = jnp.einsum(
            "tqd,kd->tqk", attended_grad, key_block[:, HD:], preferred_element_type=wide
        )
        score_grad = (probs * (prob_grad - delta[..., None])).astype(low)
        query_grad = query_grad + 0.125 * jnp.einsum(
            "tqk,kd->tqd", score_grad, key_block[:, :HD], preferred_element_type=wide
        )
        key_grad = 0.125 * jnp.einsum(
            "tqk,tqd->kd", score_grad, queries, preferred_element_type=wide
        )
        return (query_grad, jnp.concatenate([key_grad, value_grad], axis=-1))

    query_grad, keyval_terms = lax.scan(
        backstep, jnp.zeros((rows, groups, HD), wide), key_blocks
    )
    keyval_terms = keyval_terms.reshape(teams, rows, 2 * HD)
    keyval_sum = keyval_terms[0]
    for k in range(1, teams):
        keyval_sum = keyval_sum + swap(keyval_terms[k].astype(low), "fsdp", k).astype(wide)
    key_unrotated = rotate(keyval_sum[:, :HD], cosine_table, -sine_table)
    query_unrotated = rotate(query_grad, cosine_table, -sine_table).reshape(rows, query_width)
    qkv_grad = jnp.concatenate(
        [query_unrotated, key_unrotated, keyval_sum[:, HD:]], axis=-1
    ).astype(low)
    qkv_grad = after(qkv_grad, mixed, down_sum)
    half_grad_one = first_sum(lambda first, end: over_cols(qkv_grad[first:end], qkv_w), rows)
    lowered_grad_one = other_sums(after(half_grad_one, gateup_owned))
    def attention_term(k):
        late_grad = after(qkv_grad, half_grad_one)
        qkv_term = over_rows(team_cols(lowered_one, k), late_grad)
        gain_term = jnp.sum(
            qkv_term * qkv_w[k * team_width : (k + 1) * team_width].astype(wide), axis=1
        ).reshape(SUB, 1, cols)
        gain_two_term = gain_grad_two[k * team_width : (k + 1) * team_width].reshape(SUB, 1, cols)
        gain_terms = jnp.concatenate([gain_term, gain_two_term], axis=1)
        out_term = over_rows(attended_low, team_cols(branch_grad, k))
        out_term = jnp.moveaxis(out_term.reshape(query_width, SUB, cols), 1, 0)
        return jnp.concatenate(
            [
                wider(qkv_term.reshape(SUB, cols, qkv_width), lanes, 2),
                wider(out_term, lanes, 2),
                wider(wider(gain_terms, lanes, 2), 16, 1),
            ],
            axis=1,
        )

    attention_sum = teams_sum(attention_term)
    lowered_grad_one = sub_sum(after(lowered_grad_one, down_owned))
    input_grad = middle_grad + norm_back(
        own_scale, own_normed, lowered_grad_one * gains[0]
    )

    attention_owned = sub_exchange(attention_sum).astype(wide)
    query_owned = jnp.concatenate(
        [attention_owned[k, :cols, :query_width] for k in range(SUB)], axis=1
    )[:, None]
    keyval_owned = jnp.sum(attention_owned[:, :cols, query_width:qkv_width], axis=0)[:, None]
    out_owned = attention_owned[:, cols : cols + query_width, :cols].reshape(
        1, SUB * query_width, cols
    )
    gains_owned = jnp.sum(
        attention_owned[:, cols + query_width : cols + query_width + 2, :cols], axis=0
    )
    gains_owned = gains_owned + sum(
        swap(gains_owned, "heads", distance) for distance in range(1, head_devices)
    )
    gains_owned = jnp.stack([gains_owned[0] / norm_gains[0].astype(wide), gains_owned[1]], axis=0)
    input_grad = after(teams_in_place(input_grad.astype(low)), block_out)
    input_grad = lax.all_gather(input_grad, "heads", axis=0, tiled=True).astype(wide)
    gateup_owned = jnp.stack(
        [
            jnp.concatenate(
                [gateup_owned[k, :cols, c * sub_units : (c + 1) * sub_units] for k in range(SUB)],
                axis=1,
            )[:, :units]
            for c in range(2)
        ],
        axis=1,
    ).astype(wide)
    down_owned = down_owned.reshape(SUB * sub_units, cols)[:units].astype(wide)
    return (
        block_out,
        input_grad,
        gains_owned,
        query_owned,
        keyval_owned,
        out_owned,
        gateup_owned,
        down_owned,
    )


def solution(mesh):
    placed = (
        P("fsdp", None),
        P(None, "fsdp"),
        P("fsdp", "heads", None),
        P("fsdp", "heads", None),
        P("heads", None, "fsdp"),
        P("fsdp", None, "heads"),
        P("heads", "fsdp"),
        P(),
        P("fsdp"),
        P("fsdp", None),
    )
    return jax.shard_map(
        on_device,
        mesh=mesh,
        in_specs=placed,
        out_specs=(
            P("fsdp", None),
            P("fsdp", None),
            P(None, "fsdp"),
            P("fsdp", "heads", None),
            P("fsdp", "heads", None),
            P("heads", None, "fsdp"),
            P("fsdp", None, "heads"),
            P("heads", "fsdp"),
        ),
        check_vma=False,
    )
```
